128 devices in a mesh: leaf: 4 (over z_hi, core), col: 32 (over y, x, z_lo).
Axes of the slice: x: 4, y: 4, z: 4 (z_hi: 2, z_lo: 2; z = z_hi * 2 + z_lo), core: 2. Of those that a mesh axis runs over, the one named last changes fastest.
Arguments:
- child_panels: bfloat16 [4, 32, 2048, 1536], P('leaf', 'col'), may hold values from -0.078125 to 0.078125
- child_fronts: float32 [4, 32, 16, 2048, 128], P('leaf', 'col'), may hold values from -0.01 to 0.09
- parent_front: float32 [4096, 4096], P('leaf', 'col'), may hold values from -0.06 to 8
- block_maps: int32 [4, 32, 16], replicated, may hold values from 0 to 31, as said below
- right_sides: float32 [4096, 128], P('leaf'), may hold values from -16 to 16
Outputs:
- factor: float32 [4096, 4096], P('leaf', 'col')
- whitened: float32 [128, 128], replicated
- condensed: float32 [4096, 128], P('leaf')
The draws below stay inside these ranges and needn't reach their ends.
Inputs may be any that keep to these rules, and one draw needn't show every extreme that they name: `block_maps`: each subtree's 16 entries are increasing and distinct, with exactly 4 of them in each range of 8 consecutive parent blocks starting at a multiple of 8.
All inputs are finite; a program needn't handle non-finite values.
Results may differ from the reference program's by a relative error of at most 0.0003.
Values sent between devices are 32-bit elements; how exact they have to be, the bound alone decides.
No kernel may reach another device: no remote copies, remote signals or barrier semaphores. Data moves between devices by JAX's collectives and lax.ppermute only.
A program may use at most 192 MiB of HBM per device.

```python
import jax
import jax.numpy as jnp
from jax import lax

BLK = 128
UB = 16
KC = 1536
NRHS = 128
NP = 1
UC = 2048
PF = 4096
RB = 8
UBL = 4
N_LEAF = 4
N_COL = 32


def draw_child_fronts(key, part):
    key = jax.random.fold_in(key, 23)
    noise_key, diag_key = jax.random.split(key)
    children = N_LEAF * N_COL
    raw_noise = jnp.clip(jax.random.normal(noise_key, (children, UC, UC), jnp.float32), -5.0, 5.0)
    diagonal = jax.random.uniform(diag_key, (children, UC), jnp.float32, 0.03, 0.09)
    symmetric = (raw_noise + jnp.swapaxes(raw_noise, 1, 2)) * (0.001 / 1.4142135)
    on_diagonal = jnp.eye(UC, dtype=bool)
    whole_front = jnp.where(on_diagonal[None, :, :], diagonal[:, :, None], symmetric)
    column_blocks = whole_front.reshape(N_LEAF, N_COL, UC, UB, BLK)
    return jnp.transpose(column_blocks, (0, 1, 3, 2, 4))


def draw_parent_front(key, part):
    key = jax.random.fold_in(key, 37)
    noise_key, diag_key = jax.random.split(key)
    raw_noise = jnp.clip(jax.random.normal(noise_key, (PF, PF), jnp.float32), -5.0, 5.0)
    diagonal = jax.random.uniform(diag_key, (PF,), jnp.float32, 4.0, 8.0)
    symmetric = (raw_noise + raw_noise.T) * (0.008 / 1.4142135)
    on_diagonal = jnp.eye(PF, dtype=bool)
    return jnp.where(on_diagonal, diagonal[:, None], symmetric)


def draw_block_maps(key, part):
    key = jax.random.fold_in(key, 11)
    ranges = N_LEAF * N_COL * N_LEAF
    subkeys = jax.random.split(key, ranges)
    orders = jax.vmap(lambda subkey: jax.random.permutation(subkey, RB))(subkeys)
    chosen = jnp.sort(orders[:, :UBL], axis=1)
    offsets = jnp.arange(ranges, dtype=jnp.int32) % N_LEAF * RB
    block_lists = (chosen + offsets[:, None]).reshape(N_LEAF, N_COL, UB)
    return block_lists.astype(jnp.int32)


def block_levels(own_key, shape, cuts, low, largest):
    loudness = 1.0
    for dim, shards_of in cuts:
        draws = jax.random.uniform(jax.random.fold_in(jax.random.fold_in(own_key, 6), dim), (shards_of,), jnp.float32, low / len(cuts), largest / len(cuts))
        loudness = loudness * jnp.repeat(jnp.exp(draws), shape[dim] // shards_of).reshape((-1,) + (1,) * (len(shape) - 1 - dim))
    return loudness


def normal_values(rng, shape, deviation, limit, cuts=(), kind=jnp.bfloat16):
    values = deviation * jax.random.normal(rng, shape, jnp.float32)
    if cuts:
        values = values * block_levels(rng, shape, cuts, -0.22, 0.18)
    return jnp.clip(values, -limit, limit).astype(kind)


def setup_inputs(seed: int = 0) -> dict:
    streams_of = jax.random.split(jax.random.key(seed), 6)
    return {
        "child_panels": normal_values(streams_of[0], (N_LEAF, N_COL, UC, KC), (0.2 / KC ** 0.5), 0.078125, ((0, 4), (1, 32))),
        "child_fronts": draw_child_fronts(jax.random.fold_in(streams_of[5], 71), 0),
        "parent_front": draw_parent_front(jax.random.fold_in(streams_of[5], 71), 0),
        "block_maps": draw_block_maps(jax.random.fold_in(streams_of[5], 71), 0),
        "right_sides": normal_values(streams_of[4], (PF, NRHS), 3.0, 16.0, ((0, 4),), jnp.float32),
    }


def reference(child_panels, child_fronts, parent_front, block_maps, right_sides):
    panels = child_panels.reshape(N_LEAF * N_COL, UC, KC)
    fronts = child_fronts.reshape(N_LEAF * N_COL, UB, UC, BLK)
    block_lists = block_maps.reshape(N_LEAF * N_COL, UB)
    within = jnp.arange(BLK, dtype=jnp.int32)

    def add_child(child, assembled):
        weights = lax.dynamic_index_in_dim(panels, child, 0, keepdims=False)
        stored = lax.dynamic_index_in_dim(fronts, child, 0, keepdims=False)
        listed = lax.dynamic_index_in_dim(block_lists, child, 0, keepdims=False)
        whole_front = jnp.transpose(stored, (1, 0, 2)).reshape(UC, UC)
        update = whole_front - jnp.dot(weights.astype(jnp.float32), weights.T.astype(jnp.float32), preferred_element_type=jnp.float32)
        target_rows = (listed[:, None] * BLK + within[None, :]).reshape(UC).astype(jnp.int32)
        return assembled.at[target_rows[:, None], target_rows[None, :]].add(update)
    assembled = lax.fori_loop(0, N_LEAF * N_COL, add_child, parent_front)
    pivot_span = NP * BLK
    pivot_factor = jnp.tril(lax.linalg.cholesky(assembled[:pivot_span, :pivot_span], symmetrize_input=False))
    lower_panel = lax.linalg.triangular_solve(pivot_factor, assembled[pivot_span:, :pivot_span], left_side=False, lower=True, transpose_a=True)
    schur_block = assembled[pivot_span:, pivot_span:] - jnp.dot(lower_panel, lower_panel.T, precision=lax.Precision.HIGHEST)
    upper_part = jnp.concatenate([pivot_factor, jnp.zeros((pivot_span, PF - pivot_span), assembled.dtype)], axis=1)
    bottom = jnp.concatenate([lower_panel, schur_block], axis=1)
    factor = jnp.concatenate([upper_part, bottom], axis=0)
    whitened = lax.linalg.triangular_solve(pivot_factor, right_sides[:pivot_span], left_side=True, lower=True)
    remaining = right_sides[pivot_span:] - jnp.dot(lower_panel, whitened, precision=lax.Precision.HIGHEST)
    condensed = jnp.concatenate([jnp.zeros((pivot_span, NRHS), right_sides.dtype), remaining], axis=0)
    return (factor, whitened, condensed)
```

```python
import functools

import jax
import jax.numpy as jnp
from jax import lax
from jax.experimental import pallas as pl
from jax.experimental.pallas import tpu as pltpu
from jax.sharding import PartitionSpec as P

BLK = 128
SUB = 32
ORDER = (2, 1, 3, 0)
AXES = ("leaf", "col")
HIGHEST = lax.Precision.HIGHEST


def links(move):
    pairs = []
    for source in range(128):
        zl, x, y = source % 2, source // 2 % 4, source // 8 % 4
        core, zh = source // 32 % 2, source // 64
        c, v, u, w = move(core, y, x, 2 * zh + zl)
        v, u, w = v % 4, u % 4, w % 4
        pairs.append((source, ((w // 2 * 2 + c) * 4 + v) * 8 + u * 2 + w % 2))
    return pairs


def along(axis, hop):
    if axis == "y":
        return links(lambda c, y, x, z: (c, y + hop, x, z))
    if axis == "x":
        return links(lambda c, y, x, z: (c, y, x + hop, z))
    return links(lambda c, y, x, z: (c, y, x, z + hop))


SIBLING = links(lambda c, y, x, z: (1 - c, y, x, z))
SWAP = links(lambda c, y, x, z: (z % 2, y, x, z // 2 * 2 + c))


def send(value, pairs):
    return lax.ppermute(value, AXES, pairs)


def product(lhs, rhs):
    return lax.dot_general(lhs, rhs, (((1,), (1,)), ((), ())), preferred_element_type=jnp.float32)


def update_columns(sub, pos, panel, front, *outs):
    step = pl.program_id(0)
    pair = pair_of(step, pos)
    lhs = panel[:, sub * SUB : (sub + 1) * SUB, :].reshape(16 * SUB, panel.shape[2])
    rhs = panel[pl.ds(2 * pair, 2)].reshape(2 * BLK, panel.shape[2])
    result = product(lhs, rhs)
    for n, out in enumerate(outs):

        @pl.when(step // 2 == n)
        def _():
            for half in range(2):
                part = result[:, half * BLK : (half + 1) * BLK].reshape(16, SUB, BLK)
                out[half] = front[half] - part


def pair_of(step, pos):
    slot = jnp.where(step < 2, ORDER[0], jnp.where(step < 4, ORDER[1], jnp.where(step < 6, ORDER[2], ORDER[3])))
    return 2 * ((pos[0] + slot) % 4) + step % 2


def update_rows(sub, pos, panel, front, out2, out1, out3, out0, scratch):
    step = pl.program_id(0)
    lhs = panel[:, sub * SUB : (sub + 1) * SUB, :].reshape(16 * SUB, panel.shape[2])
    rhs = panel[pl.ds(2 * step, 2)].reshape(2 * BLK, panel.shape[2])
    scratch[...] = product(lhs, rhs)
    for slot, out in zip(ORDER, (out2, out1, out3, out0)):
        rows = (pos[0] + slot) % 4
        for half in range(2):
            part = scratch[pl.ds(rows * 4 * SUB, 4 * SUB), half * BLK : (half + 1) * BLK]
            out[:, half] = front[half, pl.ds(4 * rows, 4)] - part.reshape(4, SUB, BLK)


def make_update(flow, sub, pos, panel, front):
    pivots = panel.shape[2]
    flops = 2 * 512 * 2048 * pivots
    cost = pl.CostEstimate(flops=flops, bytes_accessed=14 << 20, transcendentals=0)
    params = pltpu.CompilerParams(vmem_limit_bytes=32 << 20)
    whole = pl.BlockSpec((16, BLK, pivots), lambda t, pos: (0, 0, 0))
    if flow == "y":
        front_spec = pl.BlockSpec((2, 16, SUB, BLK), lambda t, pos: (pair_of(t, pos), 0, sub, 0))
        out_specs = [
            pl.BlockSpec((2, 16, SUB, BLK), functools.partial(lambda n, t, pos: (jnp.clip(t - 2 * n, 0, 1), 0, 0, 0), n))
            for n in range(4)
        ]
        shape = (4, 16, SUB, BLK)
        body, scratch = update_columns, []
    else:
        front_spec = pl.BlockSpec((2, 16, SUB, BLK), lambda t, pos: (t, 0, sub, 0))
        out_specs = [pl.BlockSpec((4, 2, SUB, BLK), lambda t, pos: (0, t, 0, 0)) for _ in range(4)]
        shape = (4, 16, SUB, BLK)
        body, scratch = update_rows, [pltpu.VMEM((16 * SUB, 2 * BLK), jnp.float32)]
    return pl.pallas_call(
        functools.partial(body, sub),
        grid_spec=pltpu.PrefetchScalarGridSpec(
            num_scalar_prefetch=1,
            grid=(8,),
            in_specs=[whole, front_spec],
            out_specs=out_specs,
            scratch_shapes=scratch,
        ),
        out_shape=[jax.ShapeDtypeStruct(shape, jnp.float32)] * 4,
        compiler_params=params,
        cost_estimate=cost,
        name="update_" + flow,
    )(pos, panel, front)


def expand_columns(pos, maps, own, behind, far, ahead, out):
    y, x, z, core = pos[0], pos[1], pos[2], pos[3]
    out[...] = jnp.zeros_like(out)
    for s, chunk in enumerate((own, behind, far, ahead)):

        def column(k, carry):
            q = maps[s, 4 * y + k] - 8 * y
            j = (q // 2 + 4 - x) % 4
            for br in range(16):
                rows = br // 4
                p = maps[s, br] - 8 * rows
                to = (rows // 2 * 2 + q % 2 + 4 - z) % 4
                kept = jnp.where(core == rows % 2, 1, 0)
                out[kept, j, to, p] += chunk[k, br]
            return carry

        lax.fori_loop(0, 4, column, 0)


def expand_rows(pos, maps, own, behind, far, ahead, out):
    y, x, z, core = pos[0], pos[1], pos[2], pos[3]
    out[...] = jnp.zeros_like(out)
    for s, chunk in enumerate((own, behind, far, ahead)):

        def row(k, carry):
            p = maps[s, 4 * z + k] - 8 * z
            for bc in range(16):
                q = maps[s, bc]
                j = (q // 2 % 4 + 4 - x) % 4
                to = (bc // 4 + 4 - y) % 4
                kept = jnp.where(core == q % 2, 1, 0)
                out[kept, j, to, p] += chunk[k, bc]
            return carry

        lax.fori_loop(0, 4, row, 0)


def make_expand(flow, pos, maps, chunks):
    vmem = pl.BlockSpec(memory_space=pltpu.VMEM)
    smem = pl.BlockSpec(memory_space=pltpu.SMEM)
    return pl.pallas_call(
        expand_columns if flow == "y" else expand_rows,
        in_specs=[smem, smem] + [vmem] * 4,
        out_specs=vmem,
        out_shape=jax.ShapeDtypeStruct((2, 4, 4, 8, SUB, BLK), jnp.float32),
        compiler_params=pltpu.CompilerParams(vmem_limit_bytes=16 << 20),
        cost_estimate=pl.CostEstimate(flops=1 << 20, bytes_accessed=16 << 20, transcendentals=0),
        name="expand_" + flow,
    )(pos, maps, *chunks)


def pivot_column(pos, my_map, panel, front, parent, out):
    out[...] = jnp.zeros_like(out)

    @pl.when(my_map[0] == 0)
    def _():
        for group in range(4):
            lhs = panel[4 * group : 4 * group + 4].reshape(4 * BLK, panel.shape[2])
            result = product(lhs, panel[0]).reshape(4, BLK, BLK)
            for n in range(4):
                out[my_map[4 * group + n]] = front[4 * group + n] - result[n]

    @pl.when(pos[4] == 0)
    def _():
        out[pl.ds(8 * pos[5], 8)] += parent[...]


def make_pivot_column(pos, my_map, panel, front, parent):
    pivots = panel.shape[2]
    smem = pl.BlockSpec(memory_space=pltpu.SMEM)
    return pl.pallas_call(
        pivot_column,
        grid=(1,),
        in_specs=[
            smem,
            smem,
            pl.BlockSpec((16, BLK, pivots), lambda t: (0, 0, 0)),
            pl.BlockSpec((pl.squeezed, 16, BLK, BLK), lambda t: (0, 0, 0, 0)),
            pl.BlockSpec((8, BLK, BLK), lambda t: (0, 0, 0)),
        ],
        out_specs=pl.BlockSpec((32, BLK, BLK), lambda t: (0, 0, 0)),
        out_shape=jax.ShapeDtypeStruct((32, BLK, BLK), jnp.float32),
        compiler_params=pltpu.CompilerParams(vmem_limit_bytes=32 << 20),
        cost_estimate=pl.CostEstimate(flops=2 * 2048 * 128 * pivots, bytes_accessed=9 << 20, transcendentals=0),
        name="pivot_column",
    )(pos, my_map, panel, front, parent)


def per_device(child_panels, child_fronts, parent_front, block_maps, right_sides):
    leaf, col = lax.axis_index("leaf"), lax.axis_index("col")
    core, y, x = leaf % 2, col // 8, col // 2 % 4
    z = leaf // 2 * 2 + col % 2
    pos = jnp.stack([y, x, z, core, col, leaf]).astype(jnp.int32)
    panel = child_panels.reshape(16, BLK, child_panels.shape[3])
    front = child_fronts.reshape(16, 16, BLK, BLK)
    flat_maps = block_maps.reshape(128, 16)

    def map_at(core, y, x, z):
        index = ((z // 2 * 2 + core) * 4 + y) * 8 + x * 2 + z % 2
        return lax.dynamic_index_in_dim(flat_maps, index, 0, keepdims=False)

    my_map = map_at(core, y, x, z)
    maps_y = jnp.stack([map_at(core, (y + d) % 4, x, z) for d in (0, 3, 2, 1)])
    maps_z = jnp.stack([map_at(core, y, x, (z + d) % 4) for d in (0, 3, 2, 1)])

    column = make_pivot_column(pos, my_map, panel, front, parent_front.reshape(8, BLK, BLK))
    rhs_rows = jnp.where((leaf == 0) & (col == 0), right_sides[0:BLK], 0.0)
    summed = lax.psum(jnp.concatenate([column.reshape(4096, BLK), rhs_rows], axis=0), AXES)

    def scatter(slots, axis):
        own = slots[0]
        return (
            own
            + send(slots[2], along(axis, 2))
            + send(slots[1], along(axis, 1))
            + send(slots[3], along(axis, -1))
        )

    pieces = []
    for sub, flow in enumerate("yzyz"):
        here = y if flow == "y" else z
        s2, s1, s3, own = make_update(flow, sub, here.reshape(1).astype(jnp.int32), panel, front)
        far = send(s2, along(flow, 2))
        behind = send(s1, along(flow, 1))
        ahead = send(s3, along(flow, -1))
        maps = maps_y if flow == "y" else maps_z
        dense = make_expand(flow, pos, maps, (own, behind, far, ahead))
        other = send(dense[0], SIBLING)
        slots = [dense[1, j] + other[j] for j in range(4)]
        partial = scatter(slots, "x")
        piece = scatter([partial[k] for k in range(4)], "z" if flow == "y" else "y")
        if flow == "z":
            piece = send(piece, SWAP)
        pieces.append(piece)
    assembled = jnp.concatenate(pieces, axis=1).reshape(1024, BLK)

    pivot_block = summed[0:BLK]
    lower = jnp.tril(lax.linalg.cholesky(pivot_block, symmetrize_input=False))
    inverse = lax.linalg.triangular_solve(
        lower, jnp.eye(BLK, dtype=jnp.float32), left_side=True, lower=True
    )
    my_rows = lax.dynamic_slice_in_dim(summed, leaf * 1024, 1024, 0)
    col_rows = lax.dynamic_slice_in_dim(summed, col * BLK, BLK, 0)
    row_global = (leaf * 1024 + jnp.arange(1024, dtype=jnp.int32))[:, None]
    solved = lax.dot_general(my_rows, inverse, (((1,), (1,)), ((), ())), precision=HIGHEST)
    own_panel = lax.dot_general(col_rows, inverse, (((1,), (1,)), ((), ())), precision=HIGHEST)
    whitened = jnp.dot(inverse, summed[4096:], precision=HIGHEST)
    schur = lax.dot_general(solved, own_panel, (((1,), (1,)), ((), ())), precision=HIGHEST)
    below = row_global >= BLK
    top = jnp.where(leaf == 0, jnp.pad(lower, ((0, 1024 - BLK), (0, 0))), 0.0)
    pivot_part = jnp.where(below, solved, top)
    base = jnp.where(below, parent_front - schur, 0.0)
    trailing = jnp.where(below, base + assembled, 0.0)
    factor = jnp.where(col == 0, pivot_part, trailing)
    condensed = jnp.where(
        below, right_sides - jnp.dot(solved, whitened, precision=HIGHEST), 0.0
    )
    return factor, whitened, condensed


def solution(mesh):
    in_specs = (
        P("leaf", "col", None, None),
        P("leaf", "col", None, None, None),
        P("leaf", "col"),
        P(),
        P("leaf", None),
    )
    out_specs = (P("leaf", "col"), P(), P("leaf", None))
    return jax.shard_map(
        per_device, mesh=mesh, in_specs=in_specs, out_specs=out_specs, check_vma=False
    )
```

```python
import functools

import jax
import jax.numpy as jnp
from jax import lax
from jax.experimental import pallas as pl
from jax.experimental.pallas import tpu as pltpu
from jax.sharding import PartitionSpec as P

BLK = 128
ORDER = (2, 1, 3, 0)
AXES = ("leaf", "col")
ROWS = {"x": (0, 48), "z": (48, 48), "y": (96, 32)}
UPDATE_VMEM = 52 << 20
EXPAND_VMEM = 56 << 20
HIGHEST = lax.Precision.HIGHEST


def links(move):
    pairs = []
    for source in range(128):
        zl, x, y = source % 2, source // 2 % 4, source // 8 % 4
        core, zh = source // 32 % 2, source // 64
        c, v, u, w = move(core, y, x, 2 * zh + zl)
        v, u, w = v % 4, u % 4, w % 4
        pairs.append((source, ((w // 2 * 2 + c) * 4 + v) * 8 + u * 2 + w % 2))
    return pairs


def along(axis, hop):
    if axis == "y":
        return links(lambda c, y, x, z: (c, y + hop, x, z))
    if axis == "x":
        return links(lambda c, y, x, z: (c, y, x + hop, z))
    return links(lambda c, y, x, z: (c, y, x, z + hop))


SIBLING = links(lambda c, y, x, z: (1 - c, y, x, z))
SWAP = links(lambda c, y, x, z: (z % 2, y, x, z // 2 * 2 + c))


PARENT = [(32 * leaf, 40 * leaf) for leaf in range(4)]
RANGE = links(lambda c, y, x, z: (y % 2, z // 2 * 2 + c, x, y // 2 * 2 + z % 2))
TURN = links(lambda c, y, x, z: (x % 2, y, z // 2 * 2 + c, x // 2 * 2 + z % 2))


def send(value, pairs):
    return lax.ppermute(value, AXES, pairs)


def product(lhs, rhs):
    return lax.dot_general(lhs, rhs, (((1,), (1,)), ((), ())), preferred_element_type=jnp.float32)


def update(pos, panel, front, pivot_front, parent, earlier, *refs):
    step = pl.program_id(0)
    pivots = panel.shape[2]
    by_column, scratch = refs[8], refs[9]
    lhs = panel[...].reshape(16 * BLK, pivots)
    rhs = panel[pl.ds(2 * step, 2)].reshape(2 * BLK, pivots)
    scratch[...] = product(lhs, rhs).reshape(16, BLK, 2 * BLK)
    for flow, me, outs in (("x", pos[1], refs[0:4]), ("z", pos[2], refs[4:8])):
        first, rows = ROWS[flow]
        for slot, out in zip(ORDER, outs):
            top = 4 * ((me + slot) % 4)
            for half in range(2):
                lanes = slice(half * BLK, (half + 1) * BLK)
                out[:, half] = (
                    front[half, pl.ds(top, 4), first : first + rows]
                    - scratch[pl.ds(top, 4), first : first + rows, lanes]
                )
    first, rows = ROWS["y"]
    for half in range(2):
        lanes = slice(half * BLK, (half + 1) * BLK)
        by_column[step // 2, pl.ds(32 * (step % 2) + 16 * half, 16)] = (
            front[half, :, first : first + rows] - scratch[:, first : first + rows, lanes]
        )

    @pl.when(step == 0)
    def _():
        column = pivot_front[...] - scratch[:, :, 0:BLK]
        corner = jnp.where(pos[4] == 1, column[0], 0.0) + jnp.where(pos[5] == 1, parent[...], 0.0)
        for n in range(4):
            by_column[n, 64:80] = column[4 * n : 4 * n + 4].reshape(16, rows, BLK)
            by_column[n, 80:84] = corner.reshape(4, rows, BLK)


def make_updates(pos, panel, front, parent_front, parent_column):
    pivots = panel.shape[2]
    rows_x, rows_z, rows_y = ROWS["x"][1], ROWS["z"][1], ROWS["y"][1]
    outs = pl.pallas_call(
        update,
        grid_spec=pltpu.PrefetchScalarGridSpec(
            num_scalar_prefetch=1,
            grid=(8,),
            in_specs=[
                pl.BlockSpec((16, BLK, pivots), lambda t, pos: (0, 0, 0)),
                pl.BlockSpec((2, 16, BLK, BLK), lambda t, pos: (t, 0, 0, 0)),
                pl.BlockSpec((pl.squeezed, 16, BLK, BLK), lambda t, pos: (0, 0, 0, 0)),
                pl.BlockSpec((BLK, BLK), lambda t, pos: (0, 0)),
                pl.BlockSpec(memory_space=pl.ANY),
            ],
            out_specs=[pl.BlockSpec((4, 2, rows_x, BLK), lambda t, pos: (0, t, 0, 0))] * 4
            + [pl.BlockSpec((4, 2, rows_z, BLK), lambda t, pos: (0, t, 0, 0))] * 4
            + [pl.BlockSpec((4, 84, rows_y, BLK), lambda t, pos: (0, 0, 0, 0))],
            scratch_shapes=[pltpu.VMEM((16, BLK, 2 * BLK), jnp.float32)],
        ),
        out_shape=[jax.ShapeDtypeStruct((4, 16, rows_x, BLK), jnp.float32)] * 4
        + [jax.ShapeDtypeStruct((4, 16, rows_z, BLK), jnp.float32)] * 4
        + [jax.ShapeDtypeStruct((4, 84, rows_y, BLK), jnp.float32)],
        compiler_params=pltpu.CompilerParams(vmem_limit_bytes=UPDATE_VMEM),
        cost_estimate=pl.CostEstimate(
            flops=2 * 2048 * 2048 * pivots, bytes_accessed=40 << 20, transcendentals=0
        ),
        name="update",
    )(pos, panel, front, front, parent_front, parent_column)
    return {
        "x": dict(zip(ORDER, [v.reshape(64, rows_x, BLK) for v in outs[0:4]])),
        "z": dict(zip(ORDER, [v.reshape(64, rows_z, BLK) for v in outs[4:8]])),
        "y": outs[8],
    }


def expand(pos, places, maps_y, maps_x, maps_z, parent, chunks_y, *refs):
    y, x, z, core = pos[0], pos[1], pos[2], pos[3]
    keep, away, out_x, out_z = refs[8:12]
    keep[0:128] = jnp.zeros_like(keep[0:128])
    away[0:128] = jnp.zeros_like(away[0:128])
    out_x[...] = jnp.zeros_like(out_x)
    out_z[...] = jnp.zeros_like(out_z)
    for s in range(4):

        def column(k, carry):
            q = maps_y[s, 4 * y + k] - 8 * y
            to = (q // 2 + 4 - x) % 4
            for zh in range(2):
                j = (zh * 2 + q % 2 + 4 - z) % 4
                at = 32 * j + 8 * to
                for n in range(4):
                    for out, side in ((keep, core), (away, 1 - core)):
                        block = 8 * zh + 4 * side + n
                        p = maps_y[s, block] - 8 * (2 * zh + side)
                        out[at + p] += chunks_y[s, 16 * k + block]
            return carry

        lax.fori_loop(0, 4, column, 0)
    has = [places[s, 0] == 0 for s in range(4)]
    for out, side in ((keep, core), (away, 1 - core)):

        def rows(n, carry):
            p = 4 * side + n
            down = [places[s, 8 * y + p] - 4 * y for s in range(4)]
            for i in range(4):
                total = parent[4 * p + i]
                for s in range(4):
                    there = has[s] & (down[s] >= 0)
                    block = chunks_y[s, 64 + 4 * jnp.maximum(down[s], 0) + i]
                    total += jnp.where(there, block, 0.0)
                out[128 + 4 * n + i] = total
            return carry

        lax.fori_loop(0, 4, rows, 0)
    for i in range(4):
        total = chunks_y[0, 80 + i] + chunks_y[1, 80 + i] + chunks_y[2, 80 + i] + chunks_y[3, 80 + i]
        keep[144 + i] = total
        away[144 + i] = total

    flows = (("x", maps_x, x, refs[0:4], out_x), ("z", maps_z, z, refs[4:8], out_z))
    for flow, maps, me, chunks, out in flows:
        for s, chunk in enumerate(chunks):

            def row(k, carry):
                p = maps[s, 4 * me + k] - 8 * me
                for block in range(16):
                    q = maps[s, block] - 8 * (block // 4)
                    if flow == "x":
                        j = block // 4
                        to = q // 4 * 2 + q % 2
                        side = q // 2 % 2
                    else:
                        j = (q // 2 + 4 - x) % 4
                        to = (block // 4 + 4 - y) % 4
                        side = q % 2
                    kept = jnp.where(core == side, 1, 0)
                    out[kept, 32 * j + 8 * to + p] += chunk[16 * k + block]
                return carry

            lax.fori_loop(0, 4, row, 0)


def make_expand(pos, places, maps, parent, chunks):
    vmem = pl.BlockSpec(memory_space=pltpu.VMEM)
    smem = pl.BlockSpec(memory_space=pltpu.SMEM)
    return pl.pallas_call(
        expand,
        in_specs=[smem] * 5 + [vmem] * 10,
        out_specs=[vmem] * 4,
        out_shape=[jax.ShapeDtypeStruct((148, ROWS["y"][1], BLK), jnp.float32)] * 2
        + [jax.ShapeDtypeStruct((2, 128, ROWS[flow][1], BLK), jnp.float32) for flow in "xz"],
        compiler_params=pltpu.CompilerParams(vmem_limit_bytes=EXPAND_VMEM),
        cost_estimate=pl.CostEstimate(flops=8 << 20, bytes_accessed=36 << 20, transcendentals=0),
        name="expand",
    )(pos, places, maps["y"], maps["x"], maps["z"], parent, *chunks)


def arrivals(slots, axis):
    return (
        send(slots[1], along(axis, 1)),
        send(slots[2], along(axis, 2)),
        send(slots[3], along(axis, -1)),
    )


def trade(value, groups):
    return lax.all_to_all(value, "col", 0, 0, axis_index_groups=groups, tiled=True)


Y_GROUPS = [[8 * k + n for k in range(4)] for n in range(8)]


def per_device(child_panels, child_fronts, parent_front, block_maps, right_sides):
    leaf, col = lax.axis_index("leaf"), lax.axis_index("col")
    core, y, x = leaf % 2, col // 8, col // 2 % 4
    z = leaf // 2 * 2 + col % 2
    panel = child_panels.reshape(16, BLK, child_panels.shape[3])
    front = child_fronts.reshape(16, 16, BLK, BLK)
    flat_maps = block_maps.reshape(128, 16)

    def map_at(core, y, x, z):
        index = ((z // 2 * 2 + core) * 4 + y) * 8 + x * 2 + z % 2
        return lax.dynamic_index_in_dim(flat_maps, index, 0, keepdims=False)

    def places_of(maps):
        hit = maps[:, :, None] == jnp.arange(32, dtype=jnp.int32)[None, None, :]
        rank = jnp.arange(1, 17, dtype=jnp.int32)[None, :, None]
        return jnp.sum(jnp.where(hit, rank, 0), axis=1).astype(jnp.int32) - 1

    my_map = map_at(core, y, x, z)
    at_corner = (leaf == 0) & (col == 0)
    pos = jnp.stack([y, x, z, core, my_map[0] == 0, at_corner]).astype(jnp.int32)
    maps = {
        "y": jnp.stack([map_at(core, d, x, z) for d in range(4)]),
        "x": jnp.stack([map_at(core, y, (x + d) % 4, z) for d in (0, 3, 2, 1)]),
        "z": jnp.stack([map_at(core, y, x, (z + d) % 4) for d in (0, 3, 2, 1)]),
    }
    places = places_of(maps["y"])
    parent_column = send(parent_front.reshape(32, 32, BLK), PARENT)

    slots = make_updates(pos, panel, front, parent_front, parent_column)
    chunks = [trade(slots["y"], Y_GROUPS)]
    for flow in "xz":
        chunks += [slots[flow][0], *arrivals(slots[flow], flow)]
    keep, away, dense_x, dense_z = make_expand(pos, places, maps, parent_column, chunks)
    halves_y = (keep + send(away, SIBLING)).reshape(148 * 32, BLK)
    halves_x = (dense_x[1] + send(dense_x[0], SIBLING)).reshape(4, 32 * 48, BLK)
    halves_z = (dense_z[1] + send(dense_z[0], SIBLING)).reshape(4, 32 * 48, BLK)

    rhs_mine = jnp.where((leaf == 0) & (col % 2 == 0), right_sides[0:BLK], 0.0)
    extra = jnp.concatenate([halves_y[128 * 32 :], rhs_mine])
    quarter = 32 * 32
    slots_y = [
        jnp.concatenate([halves_y[j * quarter : (j + 1) * quarter], extra]) for j in range(4)
    ]
    sum_x = jnp.sum(trade(halves_x, Y_GROUPS), axis=0)
    sum_y = slots_y[0] + sum(arrivals(slots_y, "z"))
    sum_z = halves_z[0] + sum(arrivals(halves_z, "x"))
    sum_x, sum_y, sum_z = lax.optimization_barrier((sum_x, sum_y, sum_z))

    extra = sum_y[quarter:]
    rhs_rows = extra[20 * 32 :]
    slots_y = [jnp.concatenate([sum_y[k * 256 : (k + 1) * 256], extra[0 : 20 * 32]]) for k in range(4)]
    slots_x = [lax.dynamic_slice_in_dim(sum_x, ((z + k) % 4) * 384, 384) for k in range(4)]
    slots_z = [sum_z[k * 384 : (k + 1) * 384] for k in range(4)]
    sum_y = slots_y[0] + sum(arrivals(slots_y, "x"))
    corner = sum_y[256 + 512 :]
    sum_x = slots_x[0] + sum(arrivals(slots_x, "z"))
    sum_z = slots_z[0] + sum(arrivals(slots_z, "y"))
    corner, sum_x, sum_y, sum_z = lax.optimization_barrier((corner, sum_x, sum_y, sum_z))
    strip_x = send(sum_x, TURN).reshape(8, 48, BLK)
    strip_z = send(sum_z, SWAP).reshape(8, 48, BLK)
    strip_y = sum_y[0:256].reshape(8, 32, BLK)
    assembled = jnp.concatenate([strip_x, strip_z, strip_y], axis=1).reshape(1024, BLK)

    mine = jnp.concatenate([sum_y[256 : 256 + 512], rhs_rows])
    other = send(mine, SIBLING)
    low, high = jnp.where(core == 0, mine, other), jnp.where(core == 0, other, mine)
    in_range = jnp.concatenate([low[0:512], high[0:512]])
    rhs_rows = low[512:]
    col_rows = lax.dynamic_index_in_dim(
        in_range.reshape(8, BLK, BLK), col % 8, 0, keepdims=False
    )
    my_rows = send(in_range, RANGE)

    lower = jnp.tril(lax.linalg.cholesky(corner, symmetrize_input=False))
    inverse = lax.linalg.triangular_solve(
        lower, jnp.eye(BLK, dtype=jnp.float32), left_side=True, lower=True
    )
    row_global = (leaf * 1024 + jnp.arange(1024, dtype=jnp.int32))[:, None]
    solved = lax.dot_general(my_rows, inverse, (((1,), (1,)), ((), ())), precision=HIGHEST)
    own_panel = lax.dot_general(col_rows, inverse, (((1,), (1,)), ((), ())), precision=HIGHEST)
    whitened = jnp.dot(inverse, rhs_rows, precision=HIGHEST)
    schur = lax.dot_general(solved, own_panel, (((1,), (1,)), ((), ())), precision=HIGHEST)
    below = row_global >= BLK
    top = jnp.where(leaf == 0, jnp.pad(lower, ((0, 1024 - BLK), (0, 0))), 0.0)
    pivot_part = jnp.where(below, solved, top)
    trailing = jnp.where(below, parent_front - schur + assembled, 0.0)
    factor = jnp.where(col == 0, pivot_part, trailing)
    condensed = jnp.where(
        below, right_sides - jnp.dot(solved, whitened, precision=HIGHEST), 0.0
    )
    return factor, whitened, condensed


def solution(mesh):
    in_specs = (
        P("leaf", "col", None, None),
        P("leaf", "col", None, None, None),
        P("leaf", "col"),
        P(),
        P("leaf", None),
    )
    out_specs = (P("leaf", "col"), P(), P("leaf", None))
    return jax.shard_map(
        per_device, mesh=mesh, in_specs=in_specs, out_specs=out_specs, check_vma=False
    )
```

```python
import functools

import jax
import jax.numpy as jnp
from jax import lax
from jax.experimental import pallas as pl
from jax.experimental.pallas import tpu as pltpu
from jax.sharding import PartitionSpec as P

BLK = 128
AXES = ("leaf", "col")
ROWS = {"x": (0, 48), "z": (48, 48), "y": (96, 32)}
UPDATE_VMEM = 52 << 20
EXPAND_VMEM = 56 << 20
HIGHEST = lax.Precision.HIGHEST


def links(move):
    pairs = []
    for source in range(128):
        zl, x, y = source % 2, source // 2 % 4, source // 8 % 4
        core, zh = source // 32 % 2, source // 64
        c, v, u, w = move(core, y, x, 2 * zh + zl)
        v, u, w = v % 4, u % 4, w % 4
        pairs.append((source, ((w // 2 * 2 + c) * 4 + v) * 8 + u * 2 + w % 2))
    return pairs


def along(axis, hop):
    if axis == "y":
        return links(lambda c, y, x, z: (c, y + hop, x, z))
    if axis == "x":
        return links(lambda c, y, x, z: (c, y, x + hop, z))
    return links(lambda c, y, x, z: (c, y, x, z + hop))


SIBLING = links(lambda c, y, x, z: (1 - c, y, x, z))
SWAP = links(lambda c, y, x, z: (z % 2, y, x, z // 2 * 2 + c))


PARENT = [(32 * leaf, 40 * leaf) for leaf in range(4)]
RANGE = links(lambda c, y, x, z: (y % 2, z // 2 * 2 + c, x, y // 2 * 2 + z % 2))
TURN = links(lambda c, y, x, z: (x % 2, y, z // 2 * 2 + c, x // 2 * 2 + z % 2))


def send(value, pairs):
    return lax.ppermute(value, AXES, pairs)


def product(lhs, rhs):
    return lax.dot_general(lhs, rhs, (((1,), (1,)), ((), ())), preferred_element_type=jnp.float32)


def update(pos, panel, front, pivot_front, parent, *refs):
    step = pl.program_id(0)
    pivots = panel.shape[2]
    by_column, scratch = refs[6], refs[7]
    lhs = panel[...].reshape(16 * BLK, pivots)
    rhs = panel[pl.ds(2 * step, 2)].reshape(2 * BLK, pivots)
    scratch[...] = product(lhs, rhs).reshape(16, BLK, 2 * BLK)
    for flow, me, outs in (("x", pos[1], refs[0:3]), ("z", pos[2], refs[3:6])):
        first, rows = ROWS[flow]
        own, plus, minus = outs
        away = 4 * ((me + 2) % 4)
        for out, at, top, count in (
            (own, 0, 4 * me, 4),
            (plus, 0, 4 * ((me + 1) % 4), 4),
            (plus, 4, away, 2),
            (minus, 0, 4 * ((me + 3) % 4), 4),
            (minus, 4, away + 2, 2),
        ):
            for half in range(2):
                lanes = slice(half * BLK, (half + 1) * BLK)
                out[at : at + count, half] = (
                    front[half, pl.ds(top, count), first : first + rows]
                    - scratch[pl.ds(top, count), first : first + rows, lanes]
                )
    first, rows = ROWS["y"]
    for half in range(2):
        lanes = slice(half * BLK, (half + 1) * BLK)
        by_column[step // 2, pl.ds(32 * (step % 2) + 16 * half, 16)] = (
            front[half, :, first : first + rows] - scratch[:, first : first + rows, lanes]
        )

    @pl.when(step == 0)
    def _():
        column = pivot_front[...] - scratch[:, :, 0:BLK]
        corner = jnp.where(pos[4] == 1, column[0], 0.0) + jnp.where(pos[5] == 1, parent[...], 0.0)
        for n in range(4):
            by_column[n, 64:80] = column[4 * n : 4 * n + 4].reshape(16, rows, BLK)
            by_column[n, 80:84] = corner.reshape(4, rows, BLK)


def make_updates(pos, panel, front, parent_front):
    pivots = panel.shape[2]
    rows_x, rows_z, rows_y = ROWS["x"][1], ROWS["z"][1], ROWS["y"][1]
    outs = pl.pallas_call(
        update,
        grid_spec=pltpu.PrefetchScalarGridSpec(
            num_scalar_prefetch=1,
            grid=(8,),
            in_specs=[
                pl.BlockSpec((16, BLK, pivots), lambda t, pos: (0, 0, 0)),
                pl.BlockSpec((2, 16, BLK, BLK), lambda t, pos: (t, 0, 0, 0)),
                pl.BlockSpec((pl.squeezed, 16, BLK, BLK), lambda t, pos: (0, 0, 0, 0)),
                pl.BlockSpec((BLK, BLK), lambda t, pos: (0, 0)),
            ],
            out_specs=[
                pl.BlockSpec((count, 2, rows, BLK), lambda t, pos: (0, t, 0, 0))
                for rows in (rows_x, rows_z)
                for count in (4, 6, 6)
            ]
            + [pl.BlockSpec((4, 84, rows_y, BLK), lambda t, pos: (0, 0, 0, 0))],
            scratch_shapes=[pltpu.VMEM((16, BLK, 2 * BLK), jnp.float32)],
        ),
        out_shape=[
            jax.ShapeDtypeStruct((count, 16, rows, BLK), jnp.float32)
            for rows in (rows_x, rows_z)
            for count in (4, 6, 6)
        ]
        + [jax.ShapeDtypeStruct((4, 84, rows_y, BLK), jnp.float32)],
        compiler_params=pltpu.CompilerParams(vmem_limit_bytes=UPDATE_VMEM),
        cost_estimate=pl.CostEstimate(
            flops=2 * 2048 * 2048 * pivots, bytes_accessed=40 << 20, transcendentals=0
        ),
        name="update",
    )(pos, panel, front, front, parent_front)
    flat = [v.reshape(-1, v.shape[2], BLK) for v in outs[0:6]]
    return {"x": flat[0:3], "z": flat[3:6], "y": outs[6]}


def add_rows(flow, pos, maps, out, chunks):
    y, x, z, core = pos[0], pos[1], pos[2], pos[3]
    me = x if flow == "x" else z
    for s, chunk, first, count in chunks:

        def row(k, carry):
            p = maps[s, 4 * me + first + k] - 8 * me
            for block in range(16):
                q = maps[s, block] - 8 * (block // 4)
                if flow == "x":
                    j = (q // 4 * 2 + q % 2 + 4 - z) % 4
                    to = block // 4
                    side = q // 2 % 2
                else:
                    j = (block // 4 + 4 - y) % 4
                    to = (q // 2 + 4 - x) % 4
                    side = q % 2
                kept = jnp.where(core == side, 1, 0)
                out[kept, 32 * j + 8 * to + p] += chunk[16 * k + block]
            return carry

        lax.fori_loop(0, count, row, 0)


def expand_near(pos, maps_x, maps_z, parent, *refs):
    for flow, maps, chunks, out in (
        ("x", maps_x, refs[0:3], refs[6]),
        ("z", maps_z, refs[3:6], refs[7]),
    ):
        out[...] = jnp.zeros_like(out)
        own, behind, ahead = chunks
        add_rows(flow, pos, maps, out, ((0, own, 0, 4), (1, behind, 0, 4), (3, ahead, 0, 4)))


def expand_rest(pos, places, maps_y, maps_x, maps_z, parent, chunks_y, *refs):
    y, z, core = pos[0], pos[2], pos[3]
    near_x, near_z, far_x, far_z = refs[0], refs[1], refs[2:4], refs[4:6]
    keep, away, out_x, out_z = refs[6:10]
    keep[0:128] = jnp.zeros_like(keep[0:128])
    away[0:128] = jnp.zeros_like(away[0:128])
    out_x[...] = near_x[...]
    out_z[...] = near_z[...]
    add_rows("x", pos, maps_x, out_x, ((2, far_x[0], 0, 2), (2, far_x[1], 2, 2)))
    add_rows("z", pos, maps_z, out_z, ((2, far_z[0], 0, 2), (2, far_z[1], 2, 2)))
    for s in range(4):

        def column(k, carry):
            q = maps_y[s, 4 * y + k] - 8 * y
            for zh in range(2):
                at = 32 * (q // 2) + 8 * ((zh * 2 + q % 2 + 4 - z) % 4)
                for n in range(4):
                    for out, side in ((keep, core), (away, 1 - core)):
                        block = 8 * zh + 4 * side + n
                        p = maps_y[s, block] - 8 * (2 * zh + side)
                        out[at + p] += chunks_y[s, 16 * k + block]
            return carry

        lax.fori_loop(0, 4, column, 0)
    has = [places[s, 0] == 0 for s in range(4)]
    for out, side in ((keep, core), (away, 1 - core)):

        def rows(n, carry):
            p = 4 * side + n
            down = [places[s, 8 * y + p] - 4 * y for s in range(4)]
            for i in range(4):
                total = parent[4 * p + i]
                for s in range(4):
                    there = has[s] & (down[s] >= 0)
                    block = chunks_y[s, 64 + 4 * jnp.maximum(down[s], 0) + i]
                    total += jnp.where(there, block, 0.0)
                out[128 + 4 * n + i] = total
            return carry

        lax.fori_loop(0, 4, rows, 0)
    for i in range(4):
        total = chunks_y[0, 80 + i] + chunks_y[1, 80 + i] + chunks_y[2, 80 + i] + chunks_y[3, 80 + i]
        keep[144 + i] = total
        away[144 + i] = total


def make_expands(pos, places, maps, parent, own, behind, ahead):
    vmem = pl.BlockSpec(memory_space=pltpu.VMEM)
    smem = pl.BlockSpec(memory_space=pltpu.SMEM)
    params = pltpu.CompilerParams(vmem_limit_bytes=EXPAND_VMEM)
    cost = pl.CostEstimate(flops=8 << 20, bytes_accessed=30 << 20, transcendentals=0)
    dense = [jax.ShapeDtypeStruct((2, 128, ROWS[flow][1], BLK), jnp.float32) for flow in "xz"]
    near = pl.pallas_call(
        expand_near,
        in_specs=[smem] * 3 + [pl.BlockSpec(memory_space=pl.ANY)] + [vmem] * 6,
        out_specs=[vmem] * 2,
        out_shape=dense,
        compiler_params=params,
        cost_estimate=cost,
        name="expand_near",
    )(pos, maps["x"], maps["z"], parent, *(v[flow] for flow in "xz" for v in (own, behind, ahead)))

    def rest(chunks_y, far_x, far_z):
        return pl.pallas_call(
            expand_rest,
            in_specs=[smem] * 5 + [vmem] * 8,
            out_specs=[vmem] * 4,
            out_shape=[jax.ShapeDtypeStruct((148, ROWS["y"][1], BLK), jnp.float32)] * 2 + dense,
            compiler_params=params,
            cost_estimate=cost,
            name="expand_rest",
        )(pos, places, maps["y"], maps["x"], maps["z"], parent, chunks_y, *near, *far_x, *far_z)

    return rest


def arrivals(slots, axis):
    return (
        send(slots[1], along(axis, 1)),
        send(slots[2], along(axis, 2)),
        send(slots[3], along(axis, -1)),
    )


def ring_scatter(slots, axis):
    half = slots.shape[1] // 2
    behind = send(slots[2, :half], along(axis, 1))
    ahead = send(slots[2, half:], along(axis, -1))
    plus = jnp.concatenate([slots[1, :half] + behind, slots[1, half:]])
    minus = jnp.concatenate([slots[3, :half], slots[3, half:] + ahead])
    return slots[0] + send(plus, along(axis, 1)) + send(minus, along(axis, -1))


def trade(value, groups):
    return lax.all_to_all(value, "col", 0, 0, axis_index_groups=groups, tiled=True)


Y_GROUPS = [[8 * k + n for k in range(4)] for n in range(8)]
X_GROUPS = [[8 * y + 2 * k + zl for k in range(4)] for y in range(4) for zl in range(2)]


def per_device(child_panels, child_fronts, parent_front, block_maps, right_sides):
    leaf, col = lax.axis_index("leaf"), lax.axis_index("col")
    core, y, x = leaf % 2, col // 8, col // 2 % 4
    z = leaf // 2 * 2 + col % 2
    panel = child_panels.reshape(16, BLK, child_panels.shape[3])
    front = child_fronts.reshape(16, 16, BLK, BLK)
    flat_maps = block_maps.reshape(128, 16)

    def map_at(core, y, x, z):
        index = ((z // 2 * 2 + core) * 4 + y) * 8 + x * 2 + z % 2
        return lax.dynamic_index_in_dim(flat_maps, index, 0, keepdims=False)

    def places_of(maps):
        hit = maps[:, :, None] == jnp.arange(32, dtype=jnp.int32)[None, None, :]
        rank = jnp.arange(1, 17, dtype=jnp.int32)[None, :, None]
        return jnp.sum(jnp.where(hit, rank, 0), axis=1).astype(jnp.int32) - 1

    my_map = map_at(core, y, x, z)
    at_corner = (leaf == 0) & (col == 0)
    pos = jnp.stack([y, x, z, core, my_map[0] == 0, at_corner]).astype(jnp.int32)
    maps = {
        "y": jnp.stack([map_at(core, d, x, z) for d in range(4)]),
        "x": jnp.stack([map_at(core, y, (x + d) % 4, z) for d in (0, 3, 2, 1)]),
        "z": jnp.stack([map_at(core, y, x, (z + d) % 4) for d in (0, 3, 2, 1)]),
    }
    places = places_of(maps["y"])
    parent_column = send(parent_front.reshape(32, 32, BLK), PARENT)

    slots = make_updates(pos, panel, front, parent_front)
    chunks_y = trade(slots["y"], Y_GROUPS)
    own, behind, ahead, far = {}, {}, {}, {}
    for flow in "xz":
        own[flow], plus, minus = slots[flow]
        behind[flow] = send(plus, along(flow, 1))
        ahead[flow] = send(minus, along(flow, -1))
        far[flow] = (
            send(behind[flow][64:96], along(flow, 1)),
            send(ahead[flow][64:96], along(flow, -1)),
        )
    rest = make_expands(pos, places, maps, parent_column, own, behind, ahead)
    keep, away, dense_x, dense_z = rest(chunks_y, far["x"], far["z"])
    halves_y = (keep + send(away, SIBLING)).reshape(148 * 32, BLK)
    halves_x = (dense_x[1] + send(dense_x[0], SIBLING)).reshape(4, 32 * 48, BLK)
    halves_z = (dense_z[1] + send(dense_z[0], SIBLING)).reshape(4, 32 * 48, BLK)

    extra = halves_y[128 * 32 :]
    quarter = 32 * 32
    slots_y = jnp.stack(
        [jnp.concatenate([halves_y[j * quarter : (j + 1) * quarter], extra]) for j in range(4)]
    )
    sum_y = jnp.sum(trade(slots_y, X_GROUPS), axis=0)
    sum_x = ring_scatter(halves_x, "z")
    sum_z = ring_scatter(halves_z, "y")
    sum_x, sum_y, sum_z = lax.optimization_barrier((sum_x, sum_y, sum_z))

    rhs_mine = jnp.where((leaf == 0) & (col % 2 == 0), right_sides[0:BLK], 0.0)
    extra = jnp.concatenate([sum_y[quarter:], rhs_mine])
    slots_y = [jnp.concatenate([sum_y[k * 256 : (k + 1) * 256], extra]) for k in range(4)]
    slots_z = [sum_z[k * 384 : (k + 1) * 384] for k in range(4)]
    sum_y = slots_y[0] + sum(arrivals(slots_y, "z"))
    sum_x = jnp.sum(trade(sum_x.reshape(4, 384, BLK), Y_GROUPS), axis=0)
    sum_z = slots_z[0] + sum(arrivals(slots_z, "x"))
    sum_x, sum_y, sum_z = lax.optimization_barrier((sum_x, sum_y, sum_z))
    corner = sum_y[768:896]
    rhs_rows = sum_y[896:1024]
    strip_x = send(sum_x, TURN).reshape(8, 48, BLK)
    strip_z = send(sum_z, SWAP).reshape(8, 48, BLK)

    mine = jnp.concatenate([sum_y[256 : 256 + 512], rhs_rows])
    other = send(mine, SIBLING)
    low, high = jnp.where(core == 0, mine, other), jnp.where(core == 0, other, mine)
    in_range = jnp.concatenate([low[0:512], high[0:512]])
    rhs_rows = low[512:]
    col_rows = lax.dynamic_index_in_dim(
        in_range.reshape(8, BLK, BLK), col % 8, 0, keepdims=False
    )
    my_rows = send(in_range, RANGE)

    lower = jnp.tril(lax.linalg.cholesky(corner, symmetrize_input=False))
    lower, strip_x, strip_z, my_rows = lax.optimization_barrier((lower, strip_x, strip_z, my_rows))
    strip_y = sum_y[0:256].reshape(8, 32, BLK)
    assembled = jnp.concatenate([strip_x, strip_z, strip_y], axis=1).reshape(1024, BLK)
    inverse = lax.linalg.triangular_solve(
        lower, jnp.eye(BLK, dtype=jnp.float32), left_side=True, lower=True
    )
    row_global = (leaf * 1024 + jnp.arange(1024, dtype=jnp.int32))[:, None]
    solved = lax.dot_general(my_rows, inverse, (((1,), (1,)), ((), ())), precision=HIGHEST)
    own_panel = lax.dot_general(col_rows, inverse, (((1,), (1,)), ((), ())), precision=HIGHEST)
    whitened = jnp.dot(inverse, rhs_rows, precision=HIGHEST)
    schur = lax.dot_general(solved, own_panel, (((1,), (1,)), ((), ())), precision=HIGHEST)
    below = row_global >= BLK
    top = jnp.where(leaf == 0, jnp.pad(lower, ((0, 1024 - BLK), (0, 0))), 0.0)
    pivot_part = jnp.where(below, solved, top)
    trailing = jnp.where(below, parent_front - schur + assembled, 0.0)
    factor = jnp.where(col == 0, pivot_part, trailing)
    condensed = jnp.where(
        below, right_sides - jnp.dot(solved, whitened, precision=HIGHEST), 0.0
    )
    return factor, whitened, condensed


def solution(mesh):
    in_specs = (
        P("leaf", "col", None, None),
        P("leaf", "col", None, None, None),
        P("leaf", "col"),
        P(),
        P("leaf", None),
    )
    out_specs = (P("leaf", "col"), P(), P("leaf", None))
    return jax.shard_map(
        per_device, mesh=mesh, in_specs=in_specs, out_specs=out_specs, check_vma=False
    )
```

```python
import functools

import jax
import jax.numpy as jnp
from jax import lax
from jax.experimental import pallas as pl
from jax.experimental.pallas import tpu as pltpu
from jax.sharding import PartitionSpec as P

BLK = 128
AXES = ("leaf", "col")
ROWS = {"x": (0, 48), "z": (48, 48), "y": (96, 32)}
UPDATE_VMEM = 52 << 20
EXPAND_VMEM = 56 << 20
HIGHEST = lax.Precision.HIGHEST


def links(move):
    pairs = []
    for source in range(128):
        zl, x, y = source % 2, source // 2 % 4, source // 8 % 4
        core, zh = source // 32 % 2, source // 64
        c, v, u, w = move(core, y, x, 2 * zh + zl)
        v, u, w = v % 4, u % 4, w % 4
        pairs.append((source, ((w // 2 * 2 + c) * 4 + v) * 8 + u * 2 + w % 2))
    return pairs


def along(axis, hop):
    if axis == "y":
        return links(lambda c, y, x, z: (c, y + hop, x, z))
    if axis == "x":
        return links(lambda c, y, x, z: (c, y, x + hop, z))
    return links(lambda c, y, x, z: (c, y, x, z + hop))


SIBLING = links(lambda c, y, x, z: (1 - c, y, x, z))
SWAP = links(lambda c, y, x, z: (z % 2, y, x, z // 2 * 2 + c))


PARENT = [(32 * leaf, 40 * leaf) for leaf in range(4)]
RANGE = links(lambda c, y, x, z: (y % 2, z // 2 * 2 + c, x, y // 2 * 2 + z % 2))
TURN = links(lambda c, y, x, z: (x % 2, y, z // 2 * 2 + c, x // 2 * 2 + z % 2))


def send(value, pairs):
    return lax.ppermute(value, AXES, pairs)


def product(lhs, rhs):
    return lax.dot_general(lhs, rhs, (((1,), (1,)), ((), ())), preferred_element_type=jnp.float32)


def update(pos, panel, front, pivot_front, earlier, *refs):
    step = pl.program_id(0)
    pivots = panel.shape[2]
    by_column, scratch = refs[6], refs[7]
    lhs = panel[...].reshape(16 * BLK, pivots)
    rhs = panel[pl.ds(2 * step, 2)].reshape(2 * BLK, pivots)
    scratch[...] = product(lhs, rhs).reshape(16, BLK, 2 * BLK)
    for flow, me, outs in (("x", pos[1], refs[0:3]), ("z", pos[2], refs[3:6])):
        first, rows = ROWS[flow]
        own, plus, minus = outs
        away = 4 * ((me + 2) % 4)
        for out, at, top, count in (
            (own, 0, 4 * me, 4),
            (plus, 0, 4 * ((me + 1) % 4), 4),
            (plus, 4, away, 2),
            (minus, 0, 4 * ((me + 3) % 4), 4),
            (minus, 4, away + 2, 2),
        ):
            for half in range(2):
                lanes = slice(half * BLK, (half + 1) * BLK)
                out[at : at + count, half] = (
                    front[half, pl.ds(top, count), first : first + rows]
                    - scratch[pl.ds(top, count), first : first + rows, lanes]
                )
    first, rows = ROWS["y"]
    for half in range(2):
        lanes = slice(half * BLK, (half + 1) * BLK)
        by_column[step // 2, pl.ds(32 * (step % 2) + 16 * half, 16)] = (
            front[half, :, first : first + rows] - scratch[:, first : first + rows, lanes]
        )

    @pl.when(step == 0)
    def _():
        column = pivot_front[...] - scratch[:, :, 0:BLK]
        for n in range(4):
            by_column[n, 64:80] = column[4 * n : 4 * n + 4].reshape(16, rows, BLK)


def corner(pos, panel, front, parent, out):
    value = front[...] - product(panel[...], panel[...])
    out[...] = jnp.where(pos[4] == 1, value, 0.0) + jnp.where(pos[5] == 1, parent[...], 0.0)


def make_corner(pos, panel, front, parent_front):
    pivots = panel.shape[2]
    return pl.pallas_call(
        corner,
        grid_spec=pltpu.PrefetchScalarGridSpec(
            num_scalar_prefetch=1,
            grid=(1,),
            in_specs=[
                pl.BlockSpec((pl.squeezed, BLK, pivots), lambda t, pos: (0, 0, 0)),
                pl.BlockSpec((pl.squeezed, pl.squeezed, BLK, BLK), lambda t, pos: (0, 0, 0, 0)),
                pl.BlockSpec((BLK, BLK), lambda t, pos: (0, 0)),
            ],
            out_specs=pl.BlockSpec((BLK, BLK), lambda t, pos: (0, 0)),
        ),
        out_shape=jax.ShapeDtypeStruct((BLK, BLK), jnp.float32),
        compiler_params=pltpu.CompilerParams(vmem_limit_bytes=16 << 20),
        cost_estimate=pl.CostEstimate(
            flops=2 * BLK * BLK * pivots, bytes_accessed=1 << 19, transcendentals=0
        ),
        name="corner",
    )(pos, panel, front, parent_front)


def make_updates(pos, panel, front, earlier):
    pivots = panel.shape[2]
    rows_x, rows_z, rows_y = ROWS["x"][1], ROWS["z"][1], ROWS["y"][1]
    outs = pl.pallas_call(
        update,
        grid_spec=pltpu.PrefetchScalarGridSpec(
            num_scalar_prefetch=1,
            grid=(8,),
            in_specs=[
                pl.BlockSpec((16, BLK, pivots), lambda t, pos: (0, 0, 0)),
                pl.BlockSpec((2, 16, BLK, BLK), lambda t, pos: (t, 0, 0, 0)),
                pl.BlockSpec((pl.squeezed, 16, BLK, BLK), lambda t, pos: (0, 0, 0, 0)),
                pl.BlockSpec(memory_space=pl.ANY),
            ],
            out_specs=[
                pl.BlockSpec((count, 2, rows, BLK), lambda t, pos: (0, t, 0, 0))
                for rows in (rows_x, rows_z)
                for count in (4, 6, 6)
            ]
            + [pl.BlockSpec((4, 80, rows_y, BLK), lambda t, pos: (0, 0, 0, 0))],
            scratch_shapes=[pltpu.VMEM((16, BLK, 2 * BLK), jnp.float32)],
        ),
        out_shape=[
            jax.ShapeDtypeStruct((count, 16, rows, BLK), jnp.float32)
            for rows in (rows_x, rows_z)
            for count in (4, 6, 6)
        ]
        + [jax.ShapeDtypeStruct((4, 80, rows_y, BLK), jnp.float32)],
        compiler_params=pltpu.CompilerParams(vmem_limit_bytes=UPDATE_VMEM),
        cost_estimate=pl.CostEstimate(
            flops=2 * 2048 * 2048 * pivots, bytes_accessed=40 << 20, transcendentals=0
        ),
        name="update",
    )(pos, panel, front, front, earlier)
    flat = [v.reshape(-1, v.shape[2], BLK) for v in outs[0:6]]
    return {"x": flat[0:3], "z": flat[3:6], "y": outs[6]}


def add_rows(flow, at, down, add, chunks):
    for s, chunk, first, count in chunks:

        def row(k, carry):
            p = down[s, first + k]
            for block in range(16):
                add(at[s, block] + p, chunk[16 * k + block])
            return carry

        lax.fori_loop(0, count, row, 0)


def expand_near(at_x, down_x, at_z, down_z, *refs):
    for flow, at, down, chunks, out in (
        ("x", at_x, down_x, refs[0:3], refs[6]),
        ("z", at_z, down_z, refs[3:6], refs[7]),
    ):
        out[...] = jnp.zeros_like(out)
        own, behind, ahead = chunks

        def add(piece, value):
            out[piece] += value

        add_rows(flow, at, down, add, ((0, own, 0, 4), (1, behind, 0, 4), (3, ahead, 0, 4)))


def expand_rest(pos, places, at_y, down_y, at_x, down_x, at_z, down_z, parent, chunks_y, *refs):
    y, core = pos[0], pos[3]
    near_x, near_z, far_x, far_z = refs[0], refs[1], refs[2:4], refs[4:6]
    keep, away, keep_x, away_x, keep_z, away_z = refs[6:12]
    for flow, at, down, near, far, kept, sent in (
        ("x", at_x, down_x, near_x, far_x, keep_x, away_x),
        ("z", at_z, down_z, near_z, far_z, keep_z, away_z),
    ):
        sent[...] = near[0:128]
        kept[...] = near[128:256]

        def add(piece, value):
            @pl.when(piece >= 128)
            def _():
                kept[piece - 128] += value

            @pl.when(piece < 128)
            def _():
                sent[piece] += value

        add_rows(flow, at, down, add, ((2, far[0], 0, 2), (2, far[1], 2, 2)))
    keep[0:128] = jnp.zeros_like(keep[0:128])
    away[0:128] = jnp.zeros_like(away[0:128])
    for s in range(4):

        def column(k, carry):
            for zh in range(2):
                at = at_y[s, 2 * k + zh]
                for n in range(4):
                    for out, side in ((keep, core), (away, 1 - core)):
                        block = 8 * zh + 4 * side + n
                        out[at + down_y[s, block]] += chunks_y[s, 16 * k + block]
            return carry

        lax.fori_loop(0, 4, column, 0)
    has = [places[s, 0] == 0 for s in range(4)]
    for out, side in ((keep, core), (away, 1 - core)):

        def rows(n, carry):
            p = 4 * side + n
            down = [places[s, 8 * y + p] - 4 * y for s in range(4)]
            for i in range(4):
                total = parent[4 * p + i]
                for s in range(4):
                    there = has[s] & (down[s] >= 0)
                    block = chunks_y[s, 64 + 4 * jnp.maximum(down[s], 0) + i]
                    total += jnp.where(there, block, 0.0)
                out[128 + 4 * n + i] = total
            return carry

        lax.fori_loop(0, 4, rows, 0)


def make_expands(pos, places, tables, parent, own, behind, ahead):
    vmem = pl.BlockSpec(memory_space=pltpu.VMEM)
    smem = pl.BlockSpec(memory_space=pltpu.SMEM)
    params = pltpu.CompilerParams(vmem_limit_bytes=EXPAND_VMEM)
    cost = pl.CostEstimate(flops=8 << 20, bytes_accessed=30 << 20, transcendentals=0)

    def pieces(count, flow):
        return jax.ShapeDtypeStruct((count, ROWS[flow][1], BLK), jnp.float32)

    near = pl.pallas_call(
        expand_near,
        in_specs=[smem] * 4 + [vmem] * 6,
        out_specs=[vmem] * 2,
        out_shape=[pieces(256, "x"), pieces(256, "z")],
        compiler_params=params,
        cost_estimate=cost,
        name="expand_near",
    )(*tables["x"], *tables["z"], *(v[flow] for flow in "xz" for v in (own, behind, ahead)))

    def rest(chunks_y, far_x, far_z):
        return pl.pallas_call(
            expand_rest,
            in_specs=[smem] * 8 + [vmem] * 8,
            out_specs=[vmem] * 6,
            out_shape=[pieces(144, "y")] * 2 + [pieces(128, "x")] * 2 + [pieces(128, "z")] * 2,
            compiler_params=params,
            cost_estimate=cost,
            name="expand_rest",
        )(
            pos, places, *tables["y"], *tables["x"], *tables["z"],
            parent, chunks_y, *near, *far_x, *far_z,
        )

    return rest


def arrivals(slots, axis):
    return (
        send(slots[1], along(axis, 1)),
        send(slots[2], along(axis, 2)),
        send(slots[3], along(axis, -1)),
    )


def ring_scatter(slots, axis):
    half = slots.shape[1] // 2
    behind = send(slots[2, :half], along(axis, 1))
    ahead = send(slots[2, half:], along(axis, -1))
    plus = jnp.concatenate([slots[1, :half] + behind, slots[1, half:]])
    minus = jnp.concatenate([slots[3, :half], slots[3, half:] + ahead])
    return slots[0] + send(plus, along(axis, 1)) + send(minus, along(axis, -1))


def trade(value, groups):
    return lax.all_to_all(value, "col", 0, 0, axis_index_groups=groups, tiled=True)


Y_GROUPS = [[8 * k + n for k in range(4)] for n in range(8)]
X_GROUPS = [[8 * y + 2 * k + zl for k in range(4)] for y in range(4) for zl in range(2)]


def per_device(child_panels, child_fronts, parent_front, block_maps, right_sides):
    leaf, col = lax.axis_index("leaf"), lax.axis_index("col")
    core, y, x = leaf % 2, col // 8, col // 2 % 4
    z = leaf // 2 * 2 + col % 2
    panel = child_panels.reshape(16, BLK, child_panels.shape[3])
    front = child_fronts.reshape(16, 16, BLK, BLK)
    flat_maps = block_maps.reshape(128, 16)

    def map_at(core, y, x, z):
        index = ((z // 2 * 2 + core) * 4 + y) * 8 + x * 2 + z % 2
        return lax.dynamic_index_in_dim(flat_maps, index, 0, keepdims=False)

    def places_of(maps):
        hit = maps[:, :, None] == jnp.arange(32, dtype=jnp.int32)[None, None, :]
        rank = jnp.arange(1, 17, dtype=jnp.int32)[None, :, None]
        return jnp.sum(jnp.where(hit, rank, 0), axis=1).astype(jnp.int32) - 1

    my_map = map_at(core, y, x, z)
    at_corner = (leaf == 0) & (col == 0)
    pos = jnp.stack([y, x, z, core, my_map[0] == 0, at_corner]).astype(jnp.int32)
    maps = {
        "y": jnp.stack([map_at(core, d, x, z) for d in range(4)]),
        "x": jnp.stack([map_at(core, y, (x + d) % 4, z) for d in (0, 3, 2, 1)]),
        "z": jnp.stack([map_at(core, y, x, (z + d) % 4) for d in (0, 3, 2, 1)]),
    }
    places = places_of(maps["y"])
    local = {flow: maps[flow] % 8 for flow in maps}
    ranges = (jnp.arange(16, dtype=jnp.int32) // 4)[None]
    q = local["x"]
    at_x = 32 * ((q // 4 * 2 + q % 2 + 4 - z) % 4) + 8 * ranges + 128 * (q // 2 % 2 == core)
    q = local["z"]
    at_z = 32 * ((ranges + 4 - y) % 4) + 8 * ((q // 2 + 4 - x) % 4) + 128 * (q % 2 == core)
    q = lax.dynamic_slice_in_dim(local["y"], 4 * y, 4, 1)[:, :, None]
    zh = jnp.arange(2, dtype=jnp.int32)[None, None]
    at_y = (32 * (q // 2) + 8 * ((zh * 2 + q % 2 + 4 - z) % 4)).reshape(4, 8)
    tables = {
        "y": (at_y.astype(jnp.int32), local["y"]),
        "x": (at_x.astype(jnp.int32), lax.dynamic_slice_in_dim(local["x"], 4 * x, 4, 1)),
        "z": (at_z.astype(jnp.int32), lax.dynamic_slice_in_dim(local["z"], 4 * z, 4, 1)),
    }
    parent_column = send(parent_front.reshape(32, 32, BLK), PARENT)
    my_corner = make_corner(pos, panel, front, parent_front)
    pivot_block = lax.psum(my_corner, AXES)

    slots = make_updates(pos, panel, front, my_corner)
    chunks_y = trade(slots["y"], Y_GROUPS)
    own, behind, ahead, far = {}, {}, {}, {}
    for flow in "xz":
        own[flow], plus, minus = slots[flow]
        behind[flow] = send(plus, along(flow, 1))
        ahead[flow] = send(minus, along(flow, -1))
        if flow == "x":
            behind["x"], parent_column = lax.optimization_barrier((behind["x"], parent_column))
        far[flow] = (
            send(behind[flow][64:96], along(flow, 1)),
            send(ahead[flow][64:96], along(flow, -1)),
        )
    rest = make_expands(pos, places, tables, parent_column, own, behind, ahead)
    keep_y, away_y, keep_x, away_x, keep_z, away_z = rest(chunks_y, far["x"], far["z"])
    halves_y = (keep_y + send(away_y, SIBLING)).reshape(144 * 32, BLK)
    halves_x = (keep_x + send(away_x, SIBLING)).reshape(4, 32 * 48, BLK)
    halves_z = (keep_z + send(away_z, SIBLING)).reshape(4, 32 * 48, BLK)

    extra = halves_y[128 * 32 :]
    quarter = 32 * 32
    slots_y = jnp.stack(
        [jnp.concatenate([halves_y[j * quarter : (j + 1) * quarter], extra]) for j in range(4)]
    )
    sum_y = jnp.sum(trade(slots_y, X_GROUPS), axis=0)
    sum_x = ring_scatter(halves_x, "z")
    sum_z = ring_scatter(halves_z, "y")
    sum_x, sum_y, sum_z = lax.optimization_barrier((sum_x, sum_y, sum_z))

    rhs_mine = jnp.where((leaf == 0) & (col % 2 == 0), right_sides[0:BLK], 0.0)
    extra = jnp.concatenate([sum_y[quarter:], rhs_mine])
    slots_y = [jnp.concatenate([sum_y[k * 256 : (k + 1) * 256], extra]) for k in range(4)]
    slots_z = [sum_z[k * 384 : (k + 1) * 384] for k in range(4)]
    sum_y = slots_y[0] + sum(arrivals(slots_y, "z"))
    sum_x = jnp.sum(trade(sum_x.reshape(4, 384, BLK), Y_GROUPS), axis=0)
    sum_z = slots_z[0] + sum(arrivals(slots_z, "x"))
    lower = jnp.tril(lax.linalg.cholesky(pivot_block, symmetrize_input=False))
    inverse = lax.linalg.triangular_solve(
        lower, jnp.eye(BLK, dtype=jnp.float32), left_side=True, lower=True
    )
    sum_x, sum_y, sum_z, inverse = lax.optimization_barrier((sum_x, sum_y, sum_z, inverse))
    rhs_rows = sum_y[768:896]
    strip_x = send(sum_x, TURN).reshape(8, 48, BLK)
    strip_z = send(sum_z, SWAP).reshape(8, 48, BLK)

    mine = jnp.concatenate([sum_y[256 : 256 + 512], rhs_rows])
    other = send(mine, SIBLING)
    low, high = jnp.where(core == 0, mine, other), jnp.where(core == 0, other, mine)
    in_range = jnp.concatenate([low[0:512], high[0:512]])
    rhs_rows = low[512:]
    col_rows = lax.dynamic_index_in_dim(
        in_range.reshape(8, BLK, BLK), col % 8, 0, keepdims=False
    )
    my_rows = send(in_range, RANGE)

    strip_y = sum_y[0:256].reshape(8, 32, BLK)
    assembled = jnp.concatenate([strip_x, strip_z, strip_y], axis=1).reshape(1024, BLK)
    row_global = (leaf * 1024 + jnp.arange(1024, dtype=jnp.int32))[:, None]
    solved = lax.dot_general(my_rows, inverse, (((1,), (1,)), ((), ())), precision=HIGHEST)
    own_panel = lax.dot_general(col_rows, inverse, (((1,), (1,)), ((), ())), precision=HIGHEST)
    whitened = jnp.dot(inverse, rhs_rows, precision=HIGHEST)
    schur = lax.dot_general(solved, own_panel, (((1,), (1,)), ((), ())), precision=HIGHEST)
    below = row_global >= BLK
    top = jnp.where(leaf == 0, jnp.pad(lower, ((0, 1024 - BLK), (0, 0))), 0.0)
    pivot_part = jnp.where(below, solved, top)
    trailing = jnp.where(below, parent_front - schur + assembled, 0.0)
    factor = jnp.where(col == 0, pivot_part, trailing)
    condensed = jnp.where(
        below, right_sides - jnp.dot(solved, whitened, precision=HIGHEST), 0.0
    )
    return factor, whitened, condensed


def solution(mesh):
    in_specs = (
        P("leaf", "col", None, None),
        P("leaf", "col", None, None, None),
        P("leaf", "col"),
        P(),
        P("leaf", None),
    )
    out_specs = (P("leaf", "col"), P(), P("leaf", None))
    return jax.shard_map(
        per_device, mesh=mesh, in_specs=in_specs, out_specs=out_specs, check_vma=False
    )
```

```python
import functools

import jax
import jax.numpy as jnp
from jax import lax
from jax.experimental import pallas as pl
from jax.experimental.pallas import tpu as pltpu
from jax.sharding import PartitionSpec as P

BLK = 128
AXES = ("leaf", "col")
ROWS = {"x": (0, 48), "z": (48, 48), "y": (96, 32)}
UPDATE_VMEM = 52 << 20
EXPAND_VMEM = 56 << 20
HIGHEST = lax.Precision.HIGHEST


def links(move):
    pairs = []
    for source in range(128):
        zl, x, y = source % 2, source // 2 % 4, source // 8 % 4
        core, zh = source // 32 % 2, source // 64
        c, v, u, w = move(core, y, x, 2 * zh + zl)
        v, u, w = v % 4, u % 4, w % 4
        pairs.append((source, ((w // 2 * 2 + c) * 4 + v) * 8 + u * 2 + w % 2))
    return pairs


def along(axis, hop):
    if axis == "y":
        return links(lambda c, y, x, z: (c, y + hop, x, z))
    if axis == "x":
        return links(lambda c, y, x, z: (c, y, x + hop, z))
    return links(lambda c, y, x, z: (c, y, x, z + hop))


SIBLING = links(lambda c, y, x, z: (1 - c, y, x, z))
SWAP = links(lambda c, y, x, z: (z % 2, y, x, z // 2 * 2 + c))


PARENT = [(32 * leaf, 40 * leaf) for leaf in range(4)]
PARENT_SIBLING = [(32 * leaf, 32 * (leaf ^ 1) + 8 * leaf) for leaf in range(4)]
RANGE = links(lambda c, y, x, z: (y % 2, z // 2 * 2 + c, x, y // 2 * 2 + z % 2))
TURN = links(lambda c, y, x, z: (x % 2, y, z // 2 * 2 + c, x // 2 * 2 + z % 2))


def send(value, pairs):
    return lax.ppermute(value, AXES, pairs)


def product(lhs, rhs):
    return lax.dot_general(lhs, rhs, (((1,), (1,)), ((), ())), preferred_element_type=jnp.float32)


def update(pos, panel, front, pivot_front, parent, *refs):
    step = pl.program_id(0)
    pivots = panel.shape[2]
    by_column, scratch = refs[6], refs[7]
    lhs = panel[...].reshape(16 * BLK, pivots)
    rhs = panel[pl.ds(2 * step, 2)].reshape(2 * BLK, pivots)
    scratch[...] = product(lhs, rhs).reshape(16, BLK, 2 * BLK)
    for flow, me, outs in (("x", pos[1], refs[0:3]), ("z", pos[2], refs[3:6])):
        first, rows = ROWS[flow]
        own, plus, minus = outs
        away = 4 * ((me + 2) % 4)
        for out, at, top, count in (
            (own, 0, 4 * me, 4),
            (plus, 0, 4 * ((me + 1) % 4), 4),
            (plus, 4, away, 2),
            (minus, 0, 4 * ((me + 3) % 4), 4),
            (minus, 4, away + 2, 2),
        ):
            for half in range(2):
                lanes = slice(half * BLK, (half + 1) * BLK)
                out[at : at + count, half] = (
                    front[half, pl.ds(top, count), first : first + rows]
                    - scratch[pl.ds(top, count), first : first + rows, lanes]
                )
    first, rows = ROWS["y"]
    for half in range(2):
        lanes = slice(half * BLK, (half + 1) * BLK)
        by_column[step // 2, pl.ds(32 * (step % 2) + 16 * half, 16)] = (
            front[half, :, first : first + rows] - scratch[:, first : first + rows, lanes]
        )

    @pl.when(step == 0)
    def _():
        column = pivot_front[...] - scratch[:, :, 0:BLK]
        corner = jnp.where(pos[4] == 1, column[0], 0.0) + jnp.where(pos[5] == 1, parent[...], 0.0)
        for n in range(4):
            by_column[n, 64:80] = column[4 * n : 4 * n + 4].reshape(16, rows, BLK)
            by_column[n, 80:84] = corner.reshape(4, rows, BLK)


def make_updates(pos, panel, front, parent_front):
    pivots = panel.shape[2]
    rows_x, rows_z, rows_y = ROWS["x"][1], ROWS["z"][1], ROWS["y"][1]
    outs = pl.pallas_call(
        update,
        grid_spec=pltpu.PrefetchScalarGridSpec(
            num_scalar_prefetch=1,
            grid=(8,),
            in_specs=[
                pl.BlockSpec((16, BLK, pivots), lambda t, pos: (0, 0, 0)),
                pl.BlockSpec((2, 16, BLK, BLK), lambda t, pos: (t, 0, 0, 0)),
                pl.BlockSpec((pl.squeezed, 16, BLK, BLK), lambda t, pos: (0, 0, 0, 0)),
                pl.BlockSpec((BLK, BLK), lambda t, pos: (0, 0)),
            ],
            out_specs=[
                pl.BlockSpec((count, 2, rows, BLK), lambda t, pos: (0, t, 0, 0))
                for rows in (rows_x, rows_z)
                for count in (4, 6, 6)
            ]
            + [pl.BlockSpec((4, 84, rows_y, BLK), lambda t, pos: (0, 0, 0, 0))],
            scratch_shapes=[pltpu.VMEM((16, BLK, 2 * BLK), jnp.float32)],
        ),
        out_shape=[
            jax.ShapeDtypeStruct((count, 16, rows, BLK), jnp.float32)
            for rows in (rows_x, rows_z)
            for count in (4, 6, 6)
        ]
        + [jax.ShapeDtypeStruct((4, 84, rows_y, BLK), jnp.float32)],
        compiler_params=pltpu.CompilerParams(vmem_limit_bytes=UPDATE_VMEM),
        cost_estimate=pl.CostEstimate(
            flops=2 * 2048 * 2048 * pivots, bytes_accessed=40 << 20, transcendentals=0
        ),
        name="update",
    )(pos, panel, front, front, parent_front)
    flat = [v.reshape(-1, v.shape[2], BLK) for v in outs[0:6]]
    return {"x": flat[0:3], "z": flat[3:6], "y": outs[6]}


def add_rows(flow, at, down, add, chunks):
    for s, chunk, first, count in chunks:

        def row(k, carry):
            p = down[s, first + k]
            for block in range(16):
                add(at[s, block] + p, chunk[16 * k + block])
            return carry

        lax.fori_loop(0, count, row, 0)


def expand_near(at_x, down_x, at_z, down_z, *refs):
    for flow, at, down, chunks, out in (
        ("x", at_x, down_x, refs[0:3], refs[6]),
        ("z", at_z, down_z, refs[3:6], refs[7]),
    ):
        out[...] = jnp.zeros_like(out)
        own, behind, ahead = chunks

        def add(piece, value):
            out[piece] += value

        add_rows(flow, at, down, add, ((0, own, 0, 4), (1, behind, 0, 4), (3, ahead, 0, 4)))


def expand_rest(pos, places, at_y, down_y, at_x, down_x, at_z, down_z, chunks_y, *refs):
    y, core = pos[0], pos[3]
    near_x, near_z, far_x, far_z = refs[0], refs[1], refs[2:4], refs[4:6]
    keep, away, keep_x, away_x, keep_z, away_z = refs[6:12]
    for flow, at, down, near, far, kept, sent in (
        ("x", at_x, down_x, near_x, far_x, keep_x, away_x),
        ("z", at_z, down_z, near_z, far_z, keep_z, away_z),
    ):
        sent[...] = near[0:128]
        kept[...] = near[128:256]

        def add(piece, value):
            @pl.when(piece >= 128)
            def _():
                kept[piece - 128] += value

            @pl.when(piece < 128)
            def _():
                sent[piece] += value

        add_rows(flow, at, down, add, ((2, far[0], 0, 2), (2, far[1], 2, 2)))
    keep[0:128] = jnp.zeros_like(keep[0:128])
    away[0:128] = jnp.zeros_like(away[0:128])
    for s in range(4):

        def column(k, carry):
            for zh in range(2):
                at = at_y[s, 2 * k + zh]
                for n in range(4):
                    for out, side in ((keep, core), (away, 1 - core)):
                        block = 8 * zh + 4 * side + n
                        out[at + down_y[s, block]] += chunks_y[s, 16 * k + block]
            return carry

        lax.fori_loop(0, 4, column, 0)
    has = [places[s, 0] == 0 for s in range(4)]
    for out, side in ((keep, core), (away, 1 - core)):

        def rows(n, carry):
            p = 4 * side + n
            down = [places[s, 8 * y + p] - 4 * y for s in range(4)]
            for i in range(4):
                total = None
                for s in range(4):
                    there = has[s] & (down[s] >= 0)
                    block = chunks_y[s, 64 + 4 * jnp.maximum(down[s], 0) + i]
                    block = jnp.where(there, block, 0.0)
                    total = block if total is None else total + block
                out[128 + 4 * n + i] = total
            return carry

        lax.fori_loop(0, 4, rows, 0)


def make_expands(pos, places, tables, at_near, own, behind, ahead):
    vmem = pl.BlockSpec(memory_space=pltpu.VMEM)
    smem = pl.BlockSpec(memory_space=pltpu.SMEM)
    params = pltpu.CompilerParams(vmem_limit_bytes=EXPAND_VMEM)
    cost = pl.CostEstimate(flops=8 << 20, bytes_accessed=30 << 20, transcendentals=0)

    def pieces(count, flow):
        return jax.ShapeDtypeStruct((count, ROWS[flow][1], BLK), jnp.float32)

    near = pl.pallas_call(
        expand_near,
        in_specs=[smem] * 4 + [vmem] * 6,
        out_specs=[vmem] * 2,
        out_shape=[pieces(256, "x"), pieces(256, "z")],
        compiler_params=params,
        cost_estimate=cost,
        name="expand_near",
    )(at_near, tables["x"][1], *tables["z"], *(v[flow] for flow in "xz" for v in (own, behind, ahead)))

    def rest(chunks_y, far_x, far_z):
        return pl.pallas_call(
            expand_rest,
            in_specs=[smem] * 8 + [vmem] * 7,
            out_specs=[vmem] * 6,
            out_shape=[pieces(144, "y")] * 2 + [pieces(128, "x")] * 2 + [pieces(128, "z")] * 2,
            compiler_params=params,
            cost_estimate=cost,
            name="expand_rest",
        )(
            pos, places, *tables["y"], *tables["x"], *tables["z"],
            chunks_y, *near, *far_x, *far_z,
        )

    return rest


def arrivals(slots, axis):
    return (
        send(slots[1], along(axis, 1)),
        send(slots[2], along(axis, 2)),
        send(slots[3], along(axis, -1)),
    )


def ring_scatter(slots, axis):
    half = slots.shape[1] // 2
    behind = send(slots[2, :half], along(axis, 1))
    ahead = send(slots[2, half:], along(axis, -1))
    plus = jnp.concatenate([slots[1, :half] + behind, slots[1, half:]])
    minus = jnp.concatenate([slots[3, :half], slots[3, half:] + ahead])
    return slots[0] + send(plus, along(axis, 1)) + send(minus, along(axis, -1))


def trade(value, groups):
    return lax.all_to_all(value, "col", 0, 0, axis_index_groups=groups, tiled=True)


Y_GROUPS = [[8 * k + n for k in range(4)] for n in range(8)]
X_GROUPS = [[8 * y + 2 * k + zl for k in range(4)] for y in range(4) for zl in range(2)]


def per_device(child_panels, child_fronts, parent_front, block_maps, right_sides):
    leaf, col = lax.axis_index("leaf"), lax.axis_index("col")
    core, y, x = leaf % 2, col // 8, col // 2 % 4
    z = leaf // 2 * 2 + col % 2
    panel = child_panels.reshape(16, BLK, child_panels.shape[3])
    front = child_fronts.reshape(16, 16, BLK, BLK)
    flat_maps = block_maps.reshape(128, 16)

    def map_at(core, y, x, z):
        index = ((z // 2 * 2 + core) * 4 + y) * 8 + x * 2 + z % 2
        return lax.dynamic_index_in_dim(flat_maps, index, 0, keepdims=False)

    def places_of(maps):
        hit = maps[:, :, None] == jnp.arange(32, dtype=jnp.int32)[None, None, :]
        rank = jnp.arange(1, 17, dtype=jnp.int32)[None, :, None]
        return jnp.sum(jnp.where(hit, rank, 0), axis=1).astype(jnp.int32) - 1

    my_map = map_at(core, y, x, z)
    at_corner = (leaf == 0) & (col == 0)
    pos = jnp.stack([y, x, z, core, my_map[0] == 0, at_corner]).astype(jnp.int32)
    maps = {
        "y": jnp.stack([map_at(core, d, x, z) for d in range(4)]),
        "x": jnp.stack([map_at(core, y, (x + d) % 4, z) for d in (0, 3, 2, 1)]),
        "z": jnp.stack([map_at(core, y, x, (z + d) % 4) for d in (0, 3, 2, 1)]),
    }
    places = places_of(maps["y"])
    local = {flow: maps[flow] % 8 for flow in maps}
    ranges = (jnp.arange(16, dtype=jnp.int32) // 4)[None]
    q = local["x"]
    at_x = 32 * ((q // 4 * 2 + q % 2 + 4 - z) % 4) + 8 * ranges + 128 * (q // 2 % 2 == core)
    q = local["z"]
    at_z = 32 * ((ranges + 4 - y) % 4) + 8 * ((q // 2 + 4 - x) % 4) + 128 * (q % 2 == core)
    q = lax.dynamic_slice_in_dim(local["y"], 4 * y, 4, 1)[:, :, None]
    zh = jnp.arange(2, dtype=jnp.int32)[None, None]
    at_y = (32 * (q // 2) + 8 * ((zh * 2 + q % 2 + 4 - z) % 4)).reshape(4, 8)
    tables = {
        "y": (at_y.astype(jnp.int32), local["y"]),
        "x": (at_x.astype(jnp.int32), lax.dynamic_slice_in_dim(local["x"], 4 * x, 4, 1)),
        "z": (at_z.astype(jnp.int32), lax.dynamic_slice_in_dim(local["z"], 4 * z, 4, 1)),
    }

    slots = make_updates(pos, panel, front, parent_front)
    chunks_y = trade(slots["y"], Y_GROUPS)
    pivot_block = jnp.sum(chunks_y[:, 80:84], axis=0).reshape(BLK, BLK)
    pivot_block = pivot_block + send(pivot_block, SIBLING)
    at_near, pivot_block = lax.optimization_barrier((tables["x"][0], pivot_block))
    pivot_block = pivot_block + sum(arrivals([pivot_block] * 4, "z"))
    own, behind, ahead, far = {}, {}, {}, {}
    for flow in "xz":
        own[flow], plus, minus = slots[flow]
        behind[flow] = send(plus, along(flow, 1))
        ahead[flow] = send(minus, along(flow, -1))
        far[flow] = (
            send(behind[flow][64:96], along(flow, 1)),
            send(ahead[flow][64:96], along(flow, -1)),
        )
    far_z, pivot_block = lax.optimization_barrier((far["z"], pivot_block))
    rest = make_expands(pos, places, tables, at_near, own, behind, ahead)
    keep_y, away_y, keep_x, away_x, keep_z, away_z = rest(chunks_y, far["x"], far_z)
    halves_y = (keep_y + send(away_y, SIBLING)).reshape(144 * 32, BLK)
    halves_x = (keep_x + send(away_x, SIBLING)).reshape(4, 32 * 48, BLK)
    halves_z = (keep_z + send(away_z, SIBLING)).reshape(4, 32 * 48, BLK)

    pivot_rows = halves_y[128 * 32 :]
    mine = lax.dynamic_slice_in_dim(parent_front, 512 * core, 512, 0)
    theirs = lax.dynamic_slice_in_dim(parent_front, 512 * (1 - core), 512, 0)
    pivot_rows = pivot_rows + send(mine, PARENT) + send(theirs, PARENT_SIBLING)
    extra = jnp.concatenate([pivot_rows, pivot_block])
    quarter = 32 * 32
    slots_y = jnp.stack(
        [jnp.concatenate([halves_y[j * quarter : (j + 1) * quarter], extra]) for j in range(4)]
    )
    sum_y = jnp.sum(trade(slots_y, X_GROUPS), axis=0)
    sum_x = ring_scatter(halves_x, "z")
    sum_z = ring_scatter(halves_z, "y")
    sum_x, sum_y, sum_z = lax.optimization_barrier((sum_x, sum_y, sum_z))

    rhs_mine = jnp.where((leaf == 0) & (col % 2 == 0), right_sides[0:BLK], 0.0)
    pivot_block = sum_y[quarter + 512 :]
    extra = jnp.concatenate([sum_y[quarter : quarter + 512], rhs_mine])
    slots_y = [jnp.concatenate([sum_y[k * 256 : (k + 1) * 256], extra]) for k in range(4)]
    slots_z = [sum_z[k * 384 : (k + 1) * 384] for k in range(4)]
    from_z = arrivals(slots_y, "z")
    from_z, pivot_block = lax.optimization_barrier((from_z, pivot_block))
    sum_y = slots_y[0] + sum(from_z)
    sum_x = jnp.sum(trade(sum_x.reshape(4, 384, BLK), Y_GROUPS), axis=0)
    sum_z = slots_z[0] + sum(arrivals(slots_z, "x"))
    lower = jnp.tril(lax.linalg.cholesky(pivot_block, symmetrize_input=False))
    sum_x, sum_y, sum_z, lower = lax.optimization_barrier((sum_x, sum_y, sum_z, lower))
    rhs_rows = sum_y[768:896]
    strip_x = send(sum_x, TURN).reshape(8, 48, BLK)
    strip_z = send(sum_z, SWAP).reshape(8, 48, BLK)

    mine = jnp.concatenate([sum_y[256 : 256 + 512], rhs_rows])
    other = send(mine, SIBLING)
    lower, other = lax.optimization_barrier((lower, other))
    inverse = lax.linalg.triangular_solve(
        lower, jnp.eye(BLK, dtype=jnp.float32), left_side=True, lower=True
    )
    low, high = jnp.where(core == 0, mine, other), jnp.where(core == 0, other, mine)
    in_range = jnp.concatenate([low[0:512], high[0:512]])
    rhs_rows = low[512:]
    col_rows = lax.dynamic_index_in_dim(
        in_range.reshape(8, BLK, BLK), col % 8, 0, keepdims=False
    )
    my_rows = send(in_range, RANGE)

    strip_y = sum_y[0:256].reshape(8, 32, BLK)
    assembled = jnp.concatenate([strip_x, strip_z, strip_y], axis=1).reshape(1024, BLK)
    row_global = (leaf * 1024 + jnp.arange(1024, dtype=jnp.int32))[:, None]
    solved = lax.dot_general(my_rows, inverse, (((1,), (1,)), ((), ())), precision=HIGHEST)
    own_panel = lax.dot_general(col_rows, inverse, (((1,), (1,)), ((), ())), precision=HIGHEST)
    whitened = jnp.dot(inverse, rhs_rows, precision=HIGHEST)
    schur = lax.dot_general(solved, own_panel, (((1,), (1,)), ((), ())), precision=HIGHEST)
    below = row_global >= BLK
    top = jnp.where(leaf == 0, jnp.pad(lower, ((0, 1024 - BLK), (0, 0))), 0.0)
    pivot_part = jnp.where(below, solved, top)
    trailing = jnp.where(below, parent_front - schur + assembled, 0.0)
    factor = jnp.where(col == 0, pivot_part, trailing)
    condensed = jnp.where(
        below, right_sides - jnp.dot(solved, whitened, precision=HIGHEST), 0.0
    )
    return factor, whitened, condensed


def solution(mesh):
    in_specs = (
        P("leaf", "col", None, None),
        P("leaf", "col", None, None, None),
        P("leaf", "col"),
        P(),
        P("leaf", None),
    )
    out_specs = (P("leaf", "col"), P(), P("leaf", None))
    return jax.shard_map(
        per_device, mesh=mesh, in_specs=in_specs, out_specs=out_specs, check_vma=False
    )
```

```python
import functools

import jax
import jax.numpy as jnp
from jax import lax
from jax.experimental import pallas as pl
from jax.experimental.pallas import tpu as pltpu
from jax.sharding import PartitionSpec as P

BLK = 128
AXES = ("leaf", "col")
ROWS = {"x": (0, 48), "z": (48, 48), "y": (96, 32)}
UPDATE_VMEM = 52 << 20
EXPAND_VMEM = 56 << 20
HIGHEST = lax.Precision.HIGHEST


def links(move):
    pairs = []
    for source in range(128):
        zl, x, y = source % 2, source // 2 % 4, source // 8 % 4
        core, zh = source // 32 % 2, source // 64
        c, v, u, w = move(core, y, x, 2 * zh + zl)
        v, u, w = v % 4, u % 4, w % 4
        pairs.append((source, ((w // 2 * 2 + c) * 4 + v) * 8 + u * 2 + w % 2))
    return pairs


def along(axis, hop):
    if axis == "y":
        return links(lambda c, y, x, z: (c, y + hop, x, z))
    if axis == "x":
        return links(lambda c, y, x, z: (c, y, x + hop, z))
    return links(lambda c, y, x, z: (c, y, x, z + hop))


SIBLING = links(lambda c, y, x, z: (1 - c, y, x, z))
SWAP = links(lambda c, y, x, z: (z % 2, y, x, z // 2 * 2 + c))


PARENT = [(32 * leaf, 40 * leaf) for leaf in range(4)]
PARENT_SIBLING = [(32 * leaf, 32 * (leaf ^ 1) + 8 * leaf) for leaf in range(4)]
RANGE = links(lambda c, y, x, z: (y % 2, z // 2 * 2 + c, x, y // 2 * 2 + z % 2))
TURN = links(lambda c, y, x, z: (x % 2, y, z // 2 * 2 + c, x // 2 * 2 + z % 2))


def send(value, pairs):
    return lax.ppermute(value, AXES, pairs)


def product(lhs, rhs):
    return lax.dot_general(lhs, rhs, (((1,), (1,)), ((), ())), preferred_element_type=jnp.float32)


def update(pos, panel, front, pivot_front, parent, *refs):
    step = pl.program_id(0)
    pivots = panel.shape[2]
    by_column, scratch = refs[6], refs[7]
    lhs = panel[...].reshape(16 * BLK, pivots)
    rhs = panel[pl.ds(2 * step, 2)].reshape(2 * BLK, pivots)
    scratch[...] = product(lhs, rhs).reshape(16, BLK, 2 * BLK)
    for flow, me, outs in (("x", pos[1], refs[0:3]), ("z", pos[2], refs[3:6])):
        first, rows = ROWS[flow]
        own, plus, minus = outs
        away = 4 * ((me + 2) % 4)
        for out, at, top, count in (
            (own, 0, 4 * me, 4),
            (plus, 0, 4 * ((me + 1) % 4), 4),
            (plus, 4, away, 2),
            (minus, 0, 4 * ((me + 3) % 4), 4),
            (minus, 4, away + 2, 2),
        ):
            for half in range(2):
                lanes = slice(half * BLK, (half + 1) * BLK)
                out[at : at + count, half] = (
                    front[half, pl.ds(top, count), first : first + rows]
                    - scratch[pl.ds(top, count), first : first + rows, lanes]
                )
    first, rows = ROWS["y"]
    for half in range(2):
        lanes = slice(half * BLK, (half + 1) * BLK)
        by_column[step // 2, pl.ds(32 * (step % 2) + 16 * half, 16)] = (
            front[half, :, first : first + rows] - scratch[:, first : first + rows, lanes]
        )

    @pl.when(step == 0)
    def _():
        column = pivot_front[...] - scratch[:, :, 0:BLK]
        corner = jnp.where(pos[4] == 1, column[0], 0.0) + jnp.where(pos[5] == 1, parent[...], 0.0)
        for n in range(4):
            by_column[n, 64:80] = column[4 * n : 4 * n + 4].reshape(16, rows, BLK)
            by_column[n, 80:84] = corner.reshape(4, rows, BLK)


def make_updates(pos, panel, front, parent_front):
    pivots = panel.shape[2]
    rows_x, rows_z, rows_y = ROWS["x"][1], ROWS["z"][1], ROWS["y"][1]
    outs = pl.pallas_call(
        update,
        grid_spec=pltpu.PrefetchScalarGridSpec(
            num_scalar_prefetch=1,
            grid=(8,),
            in_specs=[
                pl.BlockSpec((16, BLK, pivots), lambda t, pos: (0, 0, 0)),
                pl.BlockSpec((2, 16, BLK, BLK), lambda t, pos: (t, 0, 0, 0)),
                pl.BlockSpec((pl.squeezed, 16, BLK, BLK), lambda t, pos: (0, 0, 0, 0)),
                pl.BlockSpec((BLK, BLK), lambda t, pos: (0, 0)),
            ],
            out_specs=[
                pl.BlockSpec((count, 2, rows, BLK), lambda t, pos: (0, t, 0, 0))
                for rows in (rows_x, rows_z)
                for count in (4, 6, 6)
            ]
            + [pl.BlockSpec((4, 84, rows_y, BLK), lambda t, pos: (0, 0, 0, 0))],
            scratch_shapes=[pltpu.VMEM((16, BLK, 2 * BLK), jnp.float32)],
        ),
        out_shape=[
            jax.ShapeDtypeStruct((count, 16, rows, BLK), jnp.float32)
            for rows in (rows_x, rows_z)
            for count in (4, 6, 6)
        ]
        + [jax.ShapeDtypeStruct((4, 84, rows_y, BLK), jnp.float32)],
        compiler_params=pltpu.CompilerParams(vmem_limit_bytes=UPDATE_VMEM),
        cost_estimate=pl.CostEstimate(
            flops=2 * 2048 * 2048 * pivots, bytes_accessed=40 << 20, transcendentals=0
        ),
        name="update",
    )(pos, panel, front, front, parent_front)
    flat = [v.reshape(-1, v.shape[2], BLK) for v in outs[0:6]]
    return {"x": flat[0:3], "z": flat[3:6], "y": outs[6]}


def add_rows(flow, at, down, add, chunks):
    for s, chunk, first, count in chunks:

        def row(k, carry):
            p = down[s, first + k]
            for block in range(16):
                add(at[s, block] + p, chunk[16 * k + block])
            return carry

        lax.fori_loop(0, count, row, 0)


def expand_near(at_x, down_x, at_z, down_z, *refs):
    for flow, at, down, chunks, out in (
        ("x", at_x, down_x, refs[0:3], refs[6]),
        ("z", at_z, down_z, refs[3:6], refs[7]),
    ):
        out[...] = jnp.zeros_like(out)
        own, behind, ahead = chunks

        def add(piece, value):
            out[piece] += value

        add_rows(flow, at, down, add, ((0, own, 0, 4), (1, behind, 0, 4), (3, ahead, 0, 4)))


def expand_rest(pos, places, at_y, down_y, at_x, down_x, at_z, down_z, chunks_y, *refs):
    y, core = pos[0], pos[3]
    near_x, near_z, far_x, far_z = refs[0], refs[1], refs[2:4], refs[4:6]
    keep, away, keep_x, away_x, keep_z, away_z = refs[6:12]
    for flow, at, down, near, far, kept, sent in (
        ("x", at_x, down_x, near_x, far_x, keep_x, away_x),
        ("z", at_z, down_z, near_z, far_z, keep_z, away_z),
    ):
        sent[...] = near[0:128]
        kept[...] = near[128:256]

        def add(piece, value):
            @pl.when(piece >= 128)
            def _():
                kept[piece - 128] += value

            @pl.when(piece < 128)
            def _():
                sent[piece] += value

        add_rows(flow, at, down, add, ((2, far[0], 0, 2), (2, far[1], 2, 2)))
    keep[0:128] = jnp.zeros_like(keep[0:128])
    away[0:128] = jnp.zeros_like(away[0:128])
    for s in range(4):

        def column(k, carry):
            for zh in range(2):
                at = at_y[s, 2 * k + zh]
                for n in range(4):
                    for out, side in ((keep, core), (away, 1 - core)):
                        block = 8 * zh + 4 * side + n
                        out[at + down_y[s, block]] += chunks_y[s, 16 * k + block]
            return carry

        lax.fori_loop(0, 4, column, 0)
    has = [places[s, 0] == 0 for s in range(4)]
    for out, side in ((keep, core), (away, 1 - core)):

        def rows(n, carry):
            p = 4 * side + n
            down = [places[s, 8 * y + p] - 4 * y for s in range(4)]
            for i in range(4):
                total = None
                for s in range(4):
                    there = has[s] & (down[s] >= 0)
                    block = chunks_y[s, 64 + 4 * jnp.maximum(down[s], 0) + i]
                    block = jnp.where(there, block, 0.0)
                    total = block if total is None else total + block
                out[128 + 4 * n + i] = total
            return carry

        lax.fori_loop(0, 4, rows, 0)
    for i in range(4):
        total = chunks_y[0, 80 + i] + chunks_y[1, 80 + i] + chunks_y[2, 80 + i] + chunks_y[3, 80 + i]
        keep[144 + i] = total
        away[144 + i] = total


def make_expands(pos, places, tables, own, behind, ahead):
    vmem = pl.BlockSpec(memory_space=pltpu.VMEM)
    smem = pl.BlockSpec(memory_space=pltpu.SMEM)
    params = pltpu.CompilerParams(vmem_limit_bytes=EXPAND_VMEM)
    cost = pl.CostEstimate(flops=8 << 20, bytes_accessed=30 << 20, transcendentals=0)

    def pieces(count, flow):
        return jax.ShapeDtypeStruct((count, ROWS[flow][1], BLK), jnp.float32)

    near = pl.pallas_call(
        expand_near,
        in_specs=[smem] * 4 + [vmem] * 6,
        out_specs=[vmem] * 2,
        out_shape=[pieces(256, "x"), pieces(256, "z")],
        compiler_params=params,
        cost_estimate=cost,
        name="expand_near",
    )(*tables["x"], *tables["z"], *(v[flow] for flow in "xz" for v in (own, behind, ahead)))

    def rest(chunks_y, far_x, far_z):
        return pl.pallas_call(
            expand_rest,
            in_specs=[smem] * 8 + [vmem] * 7,
            out_specs=[vmem] * 6,
            out_shape=[pieces(148, "y")] * 2 + [pieces(128, "x")] * 2 + [pieces(128, "z")] * 2,
            compiler_params=params,
            cost_estimate=cost,
            name="expand_rest",
        )(
            pos, places, *tables["y"], *tables["x"], *tables["z"],
            chunks_y, *near, *far_x, *far_z,
        )

    return rest


def arrivals(slots, axis):
    return (
        send(slots[1], along(axis, 1)),
        send(slots[2], along(axis, 2)),
        send(slots[3], along(axis, -1)),
    )


def ring_scatter(slots, axis):
    half = slots.shape[1] // 2
    behind = send(slots[2, :half], along(axis, 1))
    ahead = send(slots[2, half:], along(axis, -1))
    plus = jnp.concatenate([slots[1, :half] + behind, slots[1, half:]])
    minus = jnp.concatenate([slots[3, :half], slots[3, half:] + ahead])
    return slots[0] + send(plus, along(axis, 1)) + send(minus, along(axis, -1))


def trade(value, groups):
    return lax.all_to_all(value, "col", 0, 0, axis_index_groups=groups, tiled=True)


Y_GROUPS = [[8 * k + n for k in range(4)] for n in range(8)]
X_GROUPS = [[8 * y + 2 * k + zl for k in range(4)] for y in range(4) for zl in range(2)]


def per_device(child_panels, child_fronts, parent_front, block_maps, right_sides):
    leaf, col = lax.axis_index("leaf"), lax.axis_index("col")
    core, y, x = leaf % 2, col // 8, col // 2 % 4
    z = leaf // 2 * 2 + col % 2
    panel = child_panels.reshape(16, BLK, child_panels.shape[3])
    front = child_fronts.reshape(16, 16, BLK, BLK)
    flat_maps = block_maps.reshape(128, 16)

    def map_at(core, y, x, z):
        index = ((z // 2 * 2 + core) * 4 + y) * 8 + x * 2 + z % 2
        return lax.dynamic_index_in_dim(flat_maps, index, 0, keepdims=False)

    def places_of(maps):
        hit = maps[:, :, None] == jnp.arange(32, dtype=jnp.int32)[None, None, :]
        rank = jnp.arange(1, 17, dtype=jnp.int32)[None, :, None]
        return jnp.sum(jnp.where(hit, rank, 0), axis=1).astype(jnp.int32) - 1

    my_map = map_at(core, y, x, z)
    at_corner = (leaf == 0) & (col == 0)
    pos = jnp.stack([y, x, z, core, my_map[0] == 0, at_corner]).astype(jnp.int32)
    maps = {
        "y": jnp.stack([map_at(core, d, x, z) for d in range(4)]),
        "x": jnp.stack([map_at(core, y, (x + d) % 4, z) for d in (0, 3, 2, 1)]),
        "z": jnp.stack([map_at(core, y, x, (z + d) % 4) for d in (0, 3, 2, 1)]),
    }
    places = places_of(maps["y"])
    local = {flow: maps[flow] % 8 for flow in maps}
    ranges = (jnp.arange(16, dtype=jnp.int32) // 4)[None]
    q = local["x"]
    at_x = 32 * ((q // 4 * 2 + q % 2 + 4 - z) % 4) + 8 * ranges + 128 * (q // 2 % 2 == core)
    q = local["z"]
    at_z = 32 * ((ranges + 4 - y) % 4) + 8 * ((q // 2 + 4 - x) % 4) + 128 * (q % 2 == core)
    q = lax.dynamic_slice_in_dim(local["y"], 4 * y, 4, 1)[:, :, None]
    zh = jnp.arange(2, dtype=jnp.int32)[None, None]
    at_y = (32 * (q // 2) + 8 * ((zh * 2 + q % 2 + 4 - z) % 4)).reshape(4, 8)
    tables = {
        "y": (at_y.astype(jnp.int32), local["y"]),
        "x": (at_x.astype(jnp.int32), lax.dynamic_slice_in_dim(local["x"], 4 * x, 4, 1)),
        "z": (at_z.astype(jnp.int32), lax.dynamic_slice_in_dim(local["z"], 4 * z, 4, 1)),
    }

    slots = make_updates(pos, panel, front, parent_front)
    chunks_y = trade(slots["y"], Y_GROUPS)
    own, behind, ahead, far = {}, {}, {}, {}
    for flow in "xz":
        own[flow], plus, minus = slots[flow]
        behind[flow] = send(plus, along(flow, 1))
        ahead[flow] = send(minus, along(flow, -1))
        far[flow] = (
            send(behind[flow][64:96], along(flow, 1)),
            send(ahead[flow][64:96], along(flow, -1)),
        )
    rest = make_expands(pos, places, tables, own, behind, ahead)
    keep_y, away_y, keep_x, away_x, keep_z, away_z = rest(chunks_y, far["x"], far["z"])
    halves_y = (keep_y + send(away_y, SIBLING)).reshape(148 * 32, BLK)
    halves_x = (keep_x + send(away_x, SIBLING)).reshape(4, 32 * 48, BLK)
    halves_z = (keep_z + send(away_z, SIBLING)).reshape(4, 32 * 48, BLK)

    pivot_rows, pivot_block = halves_y[128 * 32 : 144 * 32], halves_y[144 * 32 :]
    mine = lax.dynamic_slice_in_dim(parent_front, 512 * core, 512, 0)
    theirs = lax.dynamic_slice_in_dim(parent_front, 512 * (1 - core), 512, 0)
    pivot_rows = pivot_rows + send(mine, PARENT) + send(theirs, PARENT_SIBLING)
    extra = jnp.concatenate([pivot_rows, pivot_block])
    quarter = 32 * 32
    slots_y = jnp.stack(
        [jnp.concatenate([halves_y[j * quarter : (j + 1) * quarter], extra]) for j in range(4)]
    )
    sum_y = jnp.sum(trade(slots_y, X_GROUPS), axis=0)
    sum_x = ring_scatter(halves_x, "z")
    sum_z = ring_scatter(halves_z, "y")
    sum_x, sum_y, sum_z = lax.optimization_barrier((sum_x, sum_y, sum_z))

    rhs_mine = jnp.where((leaf == 0) & (col % 2 == 0), right_sides[0:BLK], 0.0)
    extra = jnp.concatenate([sum_y[quarter:], rhs_mine])
    slots_y = [jnp.concatenate([sum_y[k * 256 : (k + 1) * 256], extra]) for k in range(4)]
    slots_z = [sum_z[k * 384 : (k + 1) * 384] for k in range(4)]
    sum_y = slots_y[0] + sum(arrivals(slots_y, "z"))
    sum_x = jnp.sum(trade(sum_x.reshape(4, 384, BLK), Y_GROUPS), axis=0)
    sum_z = slots_z[0] + sum(arrivals(slots_z, "x"))
    sum_x, sum_y, sum_z = lax.optimization_barrier((sum_x, sum_y, sum_z))
    pivot_block, rhs_rows = sum_y[768:896], sum_y[896:1024]
    strip_x = send(sum_x, TURN).reshape(8, 48, BLK)
    strip_z = send(sum_z, SWAP).reshape(8, 48, BLK)

    mine = jnp.concatenate([sum_y[256 : 256 + 512], rhs_rows])
    other = send(mine, SIBLING)
    pivot_block, strip_x, strip_z, other = lax.optimization_barrier(
        (pivot_block, strip_x, strip_z, other)
    )
    lower = jnp.tril(lax.linalg.cholesky(pivot_block, symmetrize_input=False))
    low, high = jnp.where(core == 0, mine, other), jnp.where(core == 0, other, mine)
    in_range = jnp.concatenate([low[0:512], high[0:512]])
    rhs_rows = low[512:]
    col_rows = lax.dynamic_index_in_dim(
        in_range.reshape(8, BLK, BLK), col % 8, 0, keepdims=False
    )
    my_rows = send(in_range, RANGE)
    lower, my_rows = lax.optimization_barrier((lower, my_rows))
    inverse = lax.linalg.triangular_solve(
        lower, jnp.eye(BLK, dtype=jnp.float32), left_side=True, lower=True
    )

    strip_y = sum_y[0:256].reshape(8, 32, BLK)
    assembled = jnp.concatenate([strip_x, strip_z, strip_y], axis=1).reshape(1024, BLK)
    row_global = (leaf * 1024 + jnp.arange(1024, dtype=jnp.int32))[:, None]
    solved = lax.dot_general(my_rows, inverse, (((1,), (1,)), ((), ())), precision=HIGHEST)
    own_panel = lax.dot_general(col_rows, inverse, (((1,), (1,)), ((), ())), precision=HIGHEST)
    whitened = jnp.dot(inverse, rhs_rows, precision=HIGHEST)
    schur = lax.dot_general(solved, own_panel, (((1,), (1,)), ((), ())), precision=HIGHEST)
    below = row_global >= BLK
    top = jnp.where(leaf == 0, jnp.pad(lower, ((0, 1024 - BLK), (0, 0))), 0.0)
    pivot_part = jnp.where(below, solved, top)
    trailing = jnp.where(below, parent_front - schur + assembled, 0.0)
    factor = jnp.where(col == 0, pivot_part, trailing)
    condensed = jnp.where(
        below, right_sides - jnp.dot(solved, whitened, precision=HIGHEST), 0.0
    )
    return factor, whitened, condensed


def solution(mesh):
    in_specs = (
        P("leaf", "col", None, None),
        P("leaf", "col", None, None, None),
        P("leaf", "col"),
        P(),
        P("leaf", None),
    )
    out_specs = (P("leaf", "col"), P(), P("leaf", None))
    return jax.shard_map(
        per_device, mesh=mesh, in_specs=in_specs, out_specs=out_specs, check_vma=False
    )
```

```python
import functools

import jax
import jax.numpy as jnp
from jax import lax
from jax.experimental import pallas as pl
from jax.experimental.pallas import tpu as pltpu
from jax.sharding import PartitionSpec as P

BLK = 128
AXES = ("leaf", "col")
ROWS = {"x": (0, 48), "z": (48, 48), "y": (96, 32)}
UPDATE_VMEM = 52 << 20
EXPAND_VMEM = 56 << 20
HIGHEST = lax.Precision.HIGHEST


def links(move):
    pairs = []
    for source in range(128):
        zl, x, y = source % 2, source // 2 % 4, source // 8 % 4
        core, zh = source // 32 % 2, source // 64
        c, v, u, w = move(core, y, x, 2 * zh + zl)
        v, u, w = v % 4, u % 4, w % 4
        pairs.append((source, ((w // 2 * 2 + c) * 4 + v) * 8 + u * 2 + w % 2))
    return pairs


def along(axis, hop):
    if axis == "y":
        return links(lambda c, y, x, z: (c, y + hop, x, z))
    if axis == "x":
        return links(lambda c, y, x, z: (c, y, x + hop, z))
    return links(lambda c, y, x, z: (c, y, x, z + hop))


SIBLING = links(lambda c, y, x, z: (1 - c, y, x, z))
SWAP = links(lambda c, y, x, z: (z % 2, y, x, z // 2 * 2 + c))


PARENT = [(32 * leaf, 40 * leaf) for leaf in range(4)]
PARENT_SIBLING = [(32 * leaf, 32 * (leaf ^ 1) + 8 * leaf) for leaf in range(4)]
RANGE = links(lambda c, y, x, z: (y % 2, z // 2 * 2 + c, x, y // 2 * 2 + z % 2))
TURN = links(lambda c, y, x, z: (x % 2, y, z // 2 * 2 + c, x // 2 * 2 + z % 2))


def send(value, pairs):
    return lax.ppermute(value, AXES, pairs)


def product(lhs, rhs):
    return lax.dot_general(lhs, rhs, (((1,), (1,)), ((), ())), preferred_element_type=jnp.float32)


def update(pos, panel, front, pivot_front, parent, *refs):
    step = pl.program_id(0)
    pivots = panel.shape[2]
    by_column, scratch = refs[6], refs[7]
    lhs = panel[...].reshape(16 * BLK, pivots)
    rhs = panel[pl.ds(2 * step, 2)].reshape(2 * BLK, pivots)
    scratch[...] = product(lhs, rhs).reshape(16, BLK, 2 * BLK)
    for flow, me, outs in (("x", pos[1], refs[0:3]), ("z", pos[2], refs[3:6])):
        first, rows = ROWS[flow]
        own, plus, minus = outs
        away = 4 * ((me + 2) % 4)
        for out, at, top, count in (
            (own, 0, 4 * me, 4),
            (plus, 0, 4 * ((me + 1) % 4), 4),
            (plus, 4, away, 2),
            (minus, 0, 4 * ((me + 3) % 4), 4),
            (minus, 4, away + 2, 2),
        ):
            for half in range(2):
                lanes = slice(half * BLK, (half + 1) * BLK)
                out[at : at + count, half] = (
                    front[half, pl.ds(top, count), first : first + rows]
                    - scratch[pl.ds(top, count), first : first + rows, lanes]
                )
    first, rows = ROWS["y"]
    for half in range(2):
        lanes = slice(half * BLK, (half + 1) * BLK)
        by_column[step // 2, pl.ds(32 * (step % 2) + 16 * half, 16)] = (
            front[half, :, first : first + rows] - scratch[:, first : first + rows, lanes]
        )

    @pl.when(step == 0)
    def _():
        column = pivot_front[...] - scratch[:, :, 0:BLK]
        corner = jnp.where(pos[4] == 1, column[0], 0.0) + jnp.where(pos[5] == 1, parent[...], 0.0)
        for n in range(4):
            by_column[n, 64:80] = column[4 * n : 4 * n + 4].reshape(16, rows, BLK)
            by_column[n, 80:84] = corner.reshape(4, rows, BLK)


def make_updates(pos, panel, front, parent_front):
    pivots = panel.shape[2]
    rows_x, rows_z, rows_y = ROWS["x"][1], ROWS["z"][1], ROWS["y"][1]
    outs = pl.pallas_call(
        update,
        grid_spec=pltpu.PrefetchScalarGridSpec(
            num_scalar_prefetch=1,
            grid=(8,),
            in_specs=[
                pl.BlockSpec((16, BLK, pivots), lambda t, pos: (0, 0, 0)),
                pl.BlockSpec((2, 16, BLK, BLK), lambda t, pos: (t, 0, 0, 0)),
                pl.BlockSpec((pl.squeezed, 16, BLK, BLK), lambda t, pos: (0, 0, 0, 0)),
                pl.BlockSpec((BLK, BLK), lambda t, pos: (0, 0)),
            ],
            out_specs=[
                pl.BlockSpec((count, 2, rows, BLK), lambda t, pos: (0, t, 0, 0))
                for rows in (rows_x, rows_z)
                for count in (4, 6, 6)
            ]
            + [pl.BlockSpec((4, 84, rows_y, BLK), lambda t, pos: (0, 0, 0, 0))],
            scratch_shapes=[pltpu.VMEM((16, BLK, 2 * BLK), jnp.float32)],
        ),
        out_shape=[
            jax.ShapeDtypeStruct((count, 16, rows, BLK), jnp.float32)
            for rows in (rows_x, rows_z)
            for count in (4, 6, 6)
        ]
        + [jax.ShapeDtypeStruct((4, 84, rows_y, BLK), jnp.float32)],
        compiler_params=pltpu.CompilerParams(vmem_limit_bytes=UPDATE_VMEM),
        cost_estimate=pl.CostEstimate(
            flops=2 * 2048 * 2048 * pivots, bytes_accessed=40 << 20, transcendentals=0
        ),
        name="update",
    )(pos, panel, front, front, parent_front)
    flat = [v.reshape(-1, v.shape[2], BLK) for v in outs[0:6]]
    return {"x": flat[0:3], "z": flat[3:6], "y": outs[6]}


def add_rows(flow, at, down, add, chunks):
    for s, chunk, first, count in chunks:

        def row(k, carry):
            p = down[s, first + k]
            for block in range(16):
                add(at[s, block] + p, chunk[16 * k + block])
            return carry

        lax.fori_loop(0, count, row, 0)


def expand_near(at_x, down_x, at_z, down_z, *refs):
    for flow, at, down, chunks, out in (
        ("x", at_x, down_x, refs[0:3], refs[6]),
        ("z", at_z, down_z, refs[3:6], refs[7]),
    ):
        out[...] = jnp.zeros_like(out)
        own, behind, ahead = chunks

        def add(piece, value):
            out[piece] += value

        add_rows(flow, at, down, add, ((0, own, 0, 4), (1, behind, 0, 4), (3, ahead, 0, 4)))


def expand_rest(pos, places, at_y, down_y, at_x, down_x, at_z, down_z, chunks_y, *refs):
    y, core = pos[0], pos[3]
    near_x, near_z, far_x, far_z = refs[0], refs[1], refs[2:4], refs[4:6]
    keep, away, keep_x, away_x, keep_z, away_z = refs[6:12]
    for flow, at, down, near, far, kept, sent in (
        ("x", at_x, down_x, near_x, far_x, keep_x, away_x),
        ("z", at_z, down_z, near_z, far_z, keep_z, away_z),
    ):
        sent[...] = near[0:128]
        kept[...] = near[128:256]

        def add(piece, value):
            @pl.when(piece >= 128)
            def _():
                kept[piece - 128] += value

            @pl.when(piece < 128)
            def _():
                sent[piece] += value

        add_rows(flow, at, down, add, ((2, far[0], 0, 2), (2, far[1], 2, 2)))
    keep[0:128] = jnp.zeros_like(keep[0:128])
    away[0:128] = jnp.zeros_like(away[0:128])
    for s in range(4):

        def column(k, carry):
            for zh in range(2):
                at = at_y[s, 2 * k + zh]
                for n in range(4):
                    for out, side in ((keep, core), (away, 1 - core)):
                        block = 8 * zh + 4 * side + n
                        out[at + down_y[s, block]] += chunks_y[s, 16 * k + block]
            return carry

        lax.fori_loop(0, 4, column, 0)
    has = [places[s, 0] == 0 for s in range(4)]
    for out, side in ((keep, core), (away, 1 - core)):

        def rows(n, carry):
            p = 4 * side + n
            down = [places[s, 8 * y + p] - 4 * y for s in range(4)]
            for i in range(4):
                total = None
                for s in range(4):
                    there = has[s] & (down[s] >= 0)
                    block = chunks_y[s, 64 + 4 * jnp.maximum(down[s], 0) + i]
                    block = jnp.where(there, block, 0.0)
                    total = block if total is None else total + block
                out[128 + 4 * n + i] = total
            return carry

        lax.fori_loop(0, 4, rows, 0)
    for i in range(4):
        total = chunks_y[0, 80 + i] + chunks_y[1, 80 + i] + chunks_y[2, 80 + i] + chunks_y[3, 80 + i]
        keep[144 + i] = total
        away[144 + i] = total


def make_expands(pos, places, tables, own, behind, ahead):
    vmem = pl.BlockSpec(memory_space=pltpu.VMEM)
    smem = pl.BlockSpec(memory_space=pltpu.SMEM)
    params = pltpu.CompilerParams(vmem_limit_bytes=EXPAND_VMEM)
    cost = pl.CostEstimate(flops=8 << 20, bytes_accessed=30 << 20, transcendentals=0)

    def pieces(count, flow):
        return jax.ShapeDtypeStruct((count, ROWS[flow][1], BLK), jnp.float32)

    near = pl.pallas_call(
        expand_near,
        in_specs=[smem] * 4 + [vmem] * 6,
        out_specs=[vmem] * 2,
        out_shape=[pieces(256, "x"), pieces(256, "z")],
        compiler_params=params,
        cost_estimate=cost,
        name="expand_near",
    )(*tables["x"], *tables["z"], *(v[flow] for flow in "xz" for v in (own, behind, ahead)))

    def rest(chunks_y, far_x, far_z):
        return pl.pallas_call(
            expand_rest,
            in_specs=[smem] * 8 + [vmem] * 7,
            out_specs=[vmem] * 6,
            out_shape=[pieces(148, "y")] * 2 + [pieces(128, "x")] * 2 + [pieces(128, "z")] * 2,
            compiler_params=params,
            cost_estimate=cost,
            name="expand_rest",
        )(
            pos, places, *tables["y"], *tables["x"], *tables["z"],
            chunks_y, *near, *far_x, *far_z,
        )

    return rest


def arrivals(slots, axis):
    return (
        send(slots[1], along(axis, 1)),
        send(slots[2], along(axis, 2)),
        send(slots[3], along(axis, -1)),
    )


def ring_scatter(slots, axis):
    half = slots.shape[1] // 2
    behind = send(slots[2, :half], along(axis, 1))
    ahead = send(slots[2, half:], along(axis, -1))
    plus = jnp.concatenate([slots[1, :half] + behind, slots[1, half:]])
    minus = jnp.concatenate([slots[3, :half], slots[3, half:] + ahead])
    return slots[0] + send(plus, along(axis, 1)) + send(minus, along(axis, -1))


def ring_sums(slots, extra, axis):
    half, middle = slots.shape[1] // 2, extra.shape[0] // 2
    behind = send(jnp.concatenate([slots[2, :half], extra]), along(axis, 1))
    ahead = send(jnp.concatenate([slots[2, half:], extra]), along(axis, -1))
    near = extra + behind[half:] + ahead[half:]
    plus = [slots[1, :half] + behind[:half], slots[1, half:], behind[half : half + middle]]
    minus = [slots[3, :half], slots[3, half:] + ahead[:half], ahead[half + middle :]]
    behind = send(jnp.concatenate(plus), along(axis, 1))
    ahead = send(jnp.concatenate(minus), along(axis, -1))
    total = slots[0] + behind[: 2 * half] + ahead[: 2 * half]
    return total, near + jnp.concatenate([behind[2 * half :], ahead[2 * half :]])


def trade(value, groups):
    return lax.all_to_all(value, "col", 0, 0, axis_index_groups=groups, tiled=True)


Y_GROUPS = [[8 * k + n for k in range(4)] for n in range(8)]
X_GROUPS = [[8 * y + 2 * k + zl for k in range(4)] for y in range(4) for zl in range(2)]


def per_device(child_panels, child_fronts, parent_front, block_maps, right_sides):
    leaf, col = lax.axis_index("leaf"), lax.axis_index("col")
    core, y, x = leaf % 2, col // 8, col // 2 % 4
    z = leaf // 2 * 2 + col % 2
    panel = child_panels.reshape(16, BLK, child_panels.shape[3])
    front = child_fronts.reshape(16, 16, BLK, BLK)
    flat_maps = block_maps.reshape(128, 16)

    def map_at(core, y, x, z):
        index = ((z // 2 * 2 + core) * 4 + y) * 8 + x * 2 + z % 2
        return lax.dynamic_index_in_dim(flat_maps, index, 0, keepdims=False)

    def places_of(maps):
        hit = maps[:, :, None] == jnp.arange(32, dtype=jnp.int32)[None, None, :]
        rank = jnp.arange(1, 17, dtype=jnp.int32)[None, :, None]
        return jnp.sum(jnp.where(hit, rank, 0), axis=1).astype(jnp.int32) - 1

    my_map = map_at(core, y, x, z)
    at_corner = (leaf == 0) & (col == 0)
    pos = jnp.stack([y, x, z, core, my_map[0] == 0, at_corner]).astype(jnp.int32)
    maps = {
        "y": jnp.stack([map_at(core, d, x, z) for d in range(4)]),
        "x": jnp.stack([map_at(core, y, (x + d) % 4, z) for d in (0, 3, 2, 1)]),
        "z": jnp.stack([map_at(core, y, x, (z + d) % 4) for d in (0, 3, 2, 1)]),
    }
    places = places_of(maps["y"])
    local = {flow: maps[flow] % 8 for flow in maps}
    ranges = (jnp.arange(16, dtype=jnp.int32) // 4)[None]
    q = local["x"]
    at_x = 32 * ((q // 4 * 2 + q % 2 + 4 - z) % 4) + 8 * ranges + 128 * (q // 2 % 2 == core)
    q = local["z"]
    at_z = 32 * ((ranges + 4 - y) % 4) + 8 * ((q // 2 + 4 - x) % 4) + 128 * (q % 2 == core)
    q = lax.dynamic_slice_in_dim(local["y"], 4 * y, 4, 1)[:, :, None]
    zh = jnp.arange(2, dtype=jnp.int32)[None, None]
    at_y = (32 * (q // 2) + 8 * ((zh * 2 + q % 2 + 4 - z) % 4)).reshape(4, 8)
    tables = {
        "y": (at_y.astype(jnp.int32), local["y"]),
        "x": (at_x.astype(jnp.int32), lax.dynamic_slice_in_dim(local["x"], 4 * x, 4, 1)),
        "z": (at_z.astype(jnp.int32), lax.dynamic_slice_in_dim(local["z"], 4 * z, 4, 1)),
    }

    slots = make_updates(pos, panel, front, parent_front)
    chunks_y = trade(slots["y"], Y_GROUPS)
    own, behind, ahead, far = {}, {}, {}, {}
    for flow in "xz":
        own[flow], plus, minus = slots[flow]
        behind[flow] = send(plus, along(flow, 1))
        ahead[flow] = send(minus, along(flow, -1))
        far[flow] = (
            send(behind[flow][64:96], along(flow, 1)),
            send(ahead[flow][64:96], along(flow, -1)),
        )
    rest = make_expands(pos, places, tables, own, behind, ahead)
    keep_y, away_y, keep_x, away_x, keep_z, away_z = rest(chunks_y, far["x"], far["z"])
    halves_y = (keep_y + send(away_y, SIBLING)).reshape(148 * 32, BLK)
    halves_x = (keep_x + send(away_x, SIBLING)).reshape(4, 32 * 48, BLK)
    halves_z = (keep_z + send(away_z, SIBLING)).reshape(4, 32 * 48, BLK)

    pivot_rows, pivot_block = halves_y[128 * 32 : 144 * 32], halves_y[144 * 32 :]
    mine = lax.dynamic_slice_in_dim(parent_front, 512 * core, 512, 0)
    theirs = lax.dynamic_slice_in_dim(parent_front, 512 * (1 - core), 512, 0)
    pivot_rows = pivot_rows + send(mine, PARENT) + send(theirs, PARENT_SIBLING)
    extra = jnp.concatenate([pivot_rows, pivot_block])
    quarter = 32 * 32
    slots_y = jnp.stack(
        [jnp.concatenate([halves_y[j * quarter : (j + 1) * quarter], extra]) for j in range(4)]
    )
    sum_y = jnp.sum(trade(slots_y, X_GROUPS), axis=0)
    sum_x = ring_scatter(halves_x, "z")
    sum_z = ring_scatter(halves_z, "y")
    sum_x, sum_y, sum_z = lax.optimization_barrier((sum_x, sum_y, sum_z))

    rhs_mine = jnp.where((leaf == 0) & (col % 2 == 0), right_sides[0:BLK], 0.0)
    extra = jnp.concatenate([sum_y[quarter:], rhs_mine])
    slots_y = sum_y[0:quarter].reshape(4, 256, BLK)
    slots_z = [sum_z[k * 384 : (k + 1) * 384] for k in range(4)]
    sum_y, extra = ring_sums(slots_y, extra, "z")
    sum_x = jnp.sum(trade(sum_x.reshape(4, 384, BLK), Y_GROUPS), axis=0)
    sum_z = slots_z[0] + sum(arrivals(slots_z, "x"))
    sum_x, sum_y, sum_z, extra = lax.optimization_barrier((sum_x, sum_y, sum_z, extra))
    pivot_block, rhs_rows = extra[512:640], extra[640:768]
    strip_x = send(sum_x, TURN).reshape(8, 48, BLK)
    strip_z = send(sum_z, SWAP).reshape(8, 48, BLK)

    mine = jnp.concatenate([extra[0:512], rhs_rows])
    other = send(mine, SIBLING)
    pivot_block, strip_x, strip_z, other = lax.optimization_barrier(
        (pivot_block, strip_x, strip_z, other)
    )
    lower = jnp.tril(lax.linalg.cholesky(pivot_block, symmetrize_input=False))
    low, high = jnp.where(core == 0, mine, other), jnp.where(core == 0, other, mine)
    in_range = jnp.concatenate([low[0:512], high[0:512]])
    rhs_rows = low[512:]
    col_rows = lax.dynamic_index_in_dim(
        in_range.reshape(8, BLK, BLK), col % 8, 0, keepdims=False
    )
    my_rows = send(in_range, RANGE)
    lower, my_rows = lax.optimization_barrier((lower, my_rows))
    inverse = lax.linalg.triangular_solve(
        lower, jnp.eye(BLK, dtype=jnp.float32), left_side=True, lower=True
    )

    strip_y = sum_y.reshape(8, 32, BLK)
    assembled = jnp.concatenate([strip_x, strip_z, strip_y], axis=1).reshape(1024, BLK)
    row_global = (leaf * 1024 + jnp.arange(1024, dtype=jnp.int32))[:, None]
    solved = lax.dot_general(my_rows, inverse, (((1,), (1,)), ((), ())), precision=HIGHEST)
    own_panel = lax.dot_general(col_rows, inverse, (((1,), (1,)), ((), ())), precision=HIGHEST)
    whitened = jnp.dot(inverse, rhs_rows, precision=HIGHEST)
    schur = lax.dot_general(solved, own_panel, (((1,), (1,)), ((), ())), precision=HIGHEST)
    below = row_global >= BLK
    top = jnp.where(leaf == 0, jnp.pad(lower, ((0, 1024 - BLK), (0, 0))), 0.0)
    pivot_part = jnp.where(below, solved, top)
    trailing = jnp.where(below, parent_front - schur + assembled, 0.0)
    factor = jnp.where(col == 0, pivot_part, trailing)
    condensed = jnp.where(
        below, right_sides - jnp.dot(solved, whitened, precision=HIGHEST), 0.0
    )
    return factor, whitened, condensed


def solution(mesh):
    in_specs = (
        P("leaf", "col", None, None),
        P("leaf", "col", None, None, None),
        P("leaf", "col"),
        P(),
        P("leaf", None),
    )
    out_specs = (P("leaf", "col"), P(), P("leaf", None))
    return jax.shard_map(
        per_device, mesh=mesh, in_specs=in_specs, out_specs=out_specs, check_vma=False
    )
```
